256 devices in a mesh: seq: 32 (over y, x, core), dp: 8 (over z).
Axes of the slice: x: 4, y: 4, z: 8, core: 2. Of those that a mesh axis runs over, the one named last changes fastest.
Arguments:
- saved: bfloat16 [2, 64, 4096, 768], P(None, 'dp', 'seq'), may hold values from -6 to 6
- cotangent: bfloat16 [64, 4096, 768], P('dp', 'seq'), may hold values from -6 to 6
- gain: float32 [2, 768], replicated, may hold values from 0.25 to 1.75
- weight: bfloat16 [2, 768, 3, 768], replicated, may hold values from -0.125 to 0.125
Outputs:
- grad_input: bfloat16 [64, 4096, 768], P('dp', 'seq')
- grad_weight: float32 [2, 768, 3, 768], P(None, 'seq', None, 'dp')
- grad_stats: float32 [2, 2, 768], replicated
The draws below stay inside these ranges and needn't reach their ends.
All inputs are finite; a program needn't handle non-finite values.
Results may differ from the reference program's by a relative error of at most 0.0045.
Values may be sent and summed in bfloat16 or wider, within the bound.
A program may use at most 128 MiB of HBM per device.

```python
import math
import jax
import jax.numpy as jnp
from jax import lax

C = 768
CONV_LAYERS = 2
BASE_DILATION = 16
BINS = 4096
WINDOWS = 64


def strengthened(array, key, source, target, shards_of, factor):
    def block_of(position):
        return (jnp.arange(array.shape[position]) // (array.shape[position] // shards_of)).reshape((-1,) + (1,) * (array.ndim - 1 - position))

    near = jax.random.permutation(key, shards_of)[block_of(target)]
    other_side = (block_of(target) + shards_of // 2) % shards_of
    return jnp.where((block_of(source) == near) | (block_of(source) == other_side), factor * array, array)


def level_of(own_key, extent, shards, least, high):
    def one(dim, shards_of):
        draws = jax.random.uniform(jax.random.fold_in(jax.random.fold_in(own_key, 6), dim), (shards_of,), jnp.float32, least / len(shards), high / len(shards))
        return jnp.repeat(jnp.exp(draws), extent[dim] // shards_of).reshape((-1,) + (1,) * (len(extent) - dim - 1))

    factor_of = one(*shards[0])
    for cut in shards[1:]:
        factor_of = factor_of * one(*cut)
    return factor_of


def noise(own_key, shape, spread, most, cuts=(), dtype=jnp.bfloat16):
    loudness = level_of(own_key, shape, cuts, -0.22, 0.18) if cuts else 1.0
    drawn = jax.random.normal(own_key, shape, jnp.float32) * spread * loudness
    return jnp.minimum(jnp.maximum(drawn, -most), most).astype(dtype)


def heavy_noise(rng, extent, spread, limit, cuts, heavy, kind=jnp.bfloat16):
    entries = spread * jax.random.normal(rng, extent, jnp.float32)
    if cuts:
        entries = entries * level_of(rng, extent, cuts, -0.22, 0.18)
    return jnp.clip(strengthened(entries, jax.random.fold_in(rng, 3), *heavy), -limit, limit).astype(kind)


def setup_inputs(seed: int = 0) -> dict:
    key_list = jax.random.split(jax.random.key(seed), 5)
    saved = heavy_noise(key_list[0], (CONV_LAYERS, WINDOWS, BINS, C), 1.0, 6.0, ((1, 8), (2, 32)), (2, 3, 32, 2.75))
    cotangent = heavy_noise(key_list[1], (WINDOWS, BINS, C), 1.0, 6.0, ((0, 8), (1, 32)), (1, 2, 32, 2.75))
    gain = jnp.clip(1.0 + 0.15 * jax.random.normal(key_list[2], (CONV_LAYERS, C), jnp.float32), 0.25, 1.75)
    weight = noise(key_list[3], (CONV_LAYERS, C, 3, C), (3 * C) ** -0.5, 0.125)
    return dict(saved=saved, cotangent=cotangent, gain=gain, weight=weight)


EPS = 1e-06

def front_map(features, gain_row):
    mean_sq = lax.optimization_barrier(jnp.mean(features * features, axis=-1, keepdims=True))
    normed = features * lax.rsqrt(mean_sq + EPS)
    return jax.nn.gelu(normed * gain_row)

def reference(saved, cotangent, gain, weight):
    wide = weight.shape[1]
    weight_mats = [weight[idx].transpose(1, 2, 0).reshape(3 * wide, wide) for idx in range(CONV_LAYERS)]
    scaling = 1.0 / math.sqrt(WINDOWS * BINS)

    def window_step(carry, inputs):
        grad_sums, stat_sums = carry
        window_acts, window_cot = inputs
        running = window_cot.astype(jnp.float32)
        weight_list = [None] * CONV_LAYERS
        gain_list = [None] * CONV_LAYERS
        bias_list = [None] * CONV_LAYERS
        for section_index in reversed(range(CONV_LAYERS)):
            tap_spacing = BASE_DILATION * 2 ** section_index
            act_f, backward_pull = jax.vjp(front_map, window_acts[section_index].astype(jnp.float32), gain[section_index])
            act_bf = act_f.astype(jnp.bfloat16)
            cot_bf = running.astype(jnp.bfloat16)
            act_pad = jnp.pad(act_bf, ((tap_spacing, tap_spacing), (0, 0)))
            cot_pad = jnp.pad(cot_bf, ((tap_spacing, tap_spacing), (0, 0)))
            weight_list[section_index] = jnp.stack([jnp.dot(act_pad[tap * tap_spacing:tap * tap_spacing + BINS].T, cot_bf, preferred_element_type=jnp.float32) for tap in range(3)], axis=1)
            stacked = jnp.concatenate([cot_pad[(2 - tap) * tap_spacing:(2 - tap) * tap_spacing + BINS] for tap in range(3)], axis=1)
            grad_act = jnp.dot(stacked, weight_mats[section_index], preferred_element_type=jnp.float32)
            grad_feat, grad_gain = backward_pull(grad_act)
            running = running + grad_feat
            gain_list[section_index] = grad_gain
            bias_list[section_index] = lax.optimization_barrier(jnp.sum(cot_bf.astype(jnp.float32), axis=0))
        grad_sums = grad_sums + jnp.stack(weight_list)
        stat_sums = stat_sums + jnp.stack([jnp.stack(gain_list), jnp.stack(bias_list)])
        return ((grad_sums, stat_sums), running.astype(jnp.bfloat16))
    init = (jnp.zeros((CONV_LAYERS, wide, 3, wide), jnp.float32), jnp.zeros((2, CONV_LAYERS, wide), jnp.float32))
    (grad_sums, stat_sums), grad_input = lax.scan(window_step, init, (saved.transpose(1, 0, 2, 3), cotangent))
    return (grad_input, grad_sums * scaling, stat_sums * scaling)
```

```python
import functools
import math

import jax
import jax.numpy as jnp
from jax import lax
from jax.experimental import pallas as pl
from jax.experimental.pallas import tpu as pltpu
from jax.sharding import PartitionSpec as P

EPS = 1e-06
F32 = jnp.float32
BF16 = jnp.bfloat16
MESH = pl.DeviceIdType.MESH

C = 768
W = 8
B = 128
DIL = (16, 32)
NX, NY, NZ = 4, 4, 8
UNITS = 9
ROWS = 96
K0 = math.sqrt(2.0 / math.pi)
K1 = 0.044715
SCALE = 1.0 / math.sqrt(64 * 4096)


def body(
    saved, cot, gain, weight, gin, gw, gs,
    xv, wv, c0, c1, at, gp, rstd, run, gbuf, stage,
    csend, crecv, keep, rsend, rrecv, tbuf, ysend, yrecv, yown, zb, zs, zf, zr, zown,
    sacc, sa0, sa1, sa2, sa3,
    loc_sem, out_sem, halo_s, halo_r, c_s, c_r, r_s, r_r, y_s, y_r, z_s, z_r, st_s, st_r,
):
    seq = lax.axis_index("seq")
    z = lax.axis_index("dp")
    c = lax.rem(seq, 2)
    x = lax.rem(lax.div(seq, 2), NX)
    y = lax.div(seq, 2 * NX)
    cots = (c0, c1)

    def sid(yy, xx, cc):
        return (yy * NX + xx) * 2 + cc

    def rdma(src, dst, ssem, rsem, to_seq=None, to_z=None):
        where = {"seq": seq if to_seq is None else to_seq, "dp": z if to_z is None else to_z}
        return pltpu.make_async_remote_copy(
            src_ref=src, dst_ref=dst, send_sem=ssem, recv_sem=rsem, device_id=where, device_id_type=MESH
        )

    right = lax.rem(seq + 1, 32)
    left = lax.rem(seq + 31, 32)

    ld_x = [pltpu.make_async_copy(saved.at[l], xv.at[l], loc_sem.at[l]) for l in range(2)]
    ld_c = pltpu.make_async_copy(cot, c1.at[:, pl.ds(DIL[1], B), :], loc_sem.at[2])
    ld_w = [pltpu.make_async_copy(weight.at[l], wv.at[l], loc_sem.at[3 + l]) for l in range(2)]
    ld_x[1].start()
    ld_c.start()
    ld_w[1].start()
    ld_x[0].start()
    ld_w[0].start()

    bar = pltpu.get_barrier_semaphore()
    peers = [(sid(y, x, 1 - c), z), (lax.rem(seq + 2 * c + 31, 32), z)]
    peers += [(sid(y, lax.rem(x + o, NX), c), z) for o in range(1, NX)]
    peers += [(sid(lax.rem(y + o, NY), x, c), z) for o in range(1, NY)]
    peers += [(seq, lax.rem(z + o, NZ)) for o in range(1, NZ)]
    for s, zz in peers:
        pl.semaphore_signal(bar, inc=1, device_id={"seq": s, "dp": zz}, device_id_type=MESH)
    pl.semaphore_wait(bar, len(peers))

    def halo1():
        d = DIL[1]
        return (
            rdma(cot.at[:, pl.ds(0, d), :], c1.at[:, pl.ds(B + d, d), :], halo_s.at[0], halo_r.at[0], to_seq=left),
            rdma(cot.at[:, pl.ds(B - d, d), :], c1.at[:, pl.ds(0, d), :], halo_s.at[1], halo_r.at[1], to_seq=right),
        )

    def halo0(m):
        d = DIL[0]
        ws = pl.ds(2 * m, 2)
        return (
            rdma(c0.at[ws, pl.ds(d, d), :], c0.at[ws, pl.ds(B + d, d), :], halo_s.at[2 + 2 * m], halo_r.at[2 + 2 * m], to_seq=left),
            rdma(c0.at[ws, pl.ds(B, d), :], c0.at[ws, pl.ds(0, d), :], halo_s.at[3 + 2 * m], halo_r.at[3 + 2 * m], to_seq=right),
        )

    def clear_ends(l):
        d = DIL[l]
        zero = jnp.zeros((W, d, C), BF16)

        @pl.when(seq == 0)
        def _():
            cots[l][:, pl.ds(0, d), :] = zero

        @pl.when(seq == 31)
        def _():
            cots[l][:, pl.ds(B + d, d), :] = zero

    for h in halo1():
        h.start()

    def forward(l, w):
        xt = xv[l, w].astype(F32)
        g = gain[pl.ds(l, 1), :]
        inv = lax.rsqrt(jnp.mean(xt * xt, axis=-1, keepdims=True) + EPS)
        rstd[l, w] = jnp.broadcast_to(inv, (B, 128))
        u = xt * inv * g
        u2 = u * u
        t = jnp.tanh(u * (K0 + (K0 * K1) * u2))
        h = 0.5 + 0.5 * t
        act = u * h
        gp[l, w] = h + act * (1.0 - h) * (2.0 * K0 + (6.0 * K0 * K1) * u2)
        a = act.T
        cols = pl.ds(pl.multiple_of(w * B, B), B)
        for cc in range(2):
            for t_ in range(2):
                parts = []
                for dest in range(4):
                    for other in range(4):
                        yy, xx = (other, dest) if t_ == 0 else (dest, other)
                        r0 = sid(yy, xx, cc) * 24
                        parts.append(a[r0 : r0 + 24])
                at[l, t_, cc, :, cols] = jnp.concatenate(parts, axis=0).astype(BF16)

    def kind(l, u):
        return lax.rem(u + (1 - l), 2)

    def near(t, o):
        return jnp.where(t == 0, sid(y, lax.rem(x + o, NX), c), sid(lax.rem(y + o, NY), x, c))

    def far(t, o):
        return jnp.where(t == 0, sid(lax.rem(y + o, NY), x, c), sid(y, lax.rem(x + o, NX), c))

    def tap_of(u):
        return 2 - lax.rem(lax.div(u, 3) + 1, 3)

    def core_copy(l, u):
        return rdma(csend.at[l, u], crecv.at[l, u], c_s.at[l, u], c_r.at[l, u], to_seq=sid(y, x, 1 - c))

    def ring_copy(l, u, i):
        o = 1 if i in (0, 2, 4) else 3
        return rdma(rsend.at[l, u, i], rrecv.at[l, u, i], r_s.at[l, u, i], r_r.at[l, u, i], to_seq=near(kind(l, u), o))

    def far_copy(l, u, o):
        return rdma(ysend.at[l, u, o - 1], yrecv.at[l, u, o - 1], y_s.at[l, u, o - 1], y_r.at[l, u, o - 1], to_seq=far(kind(l, u), o))

    def z_copy(l, o):
        to = lax.rem(z + o, NZ)
        return rdma(zs.at[l, to], zr.at[l, o - 1], z_s.at[l, o - 1], z_r.at[l, o - 1], to_z=to)

    def stage_a(l, u):
        d = DIL[l]
        t = kind(l, u)
        off = pl.multiple_of(lax.rem(lax.div(u, 3) + 1, 3) * d, 16)
        n0 = pl.multiple_of(lax.rem(u, 3) * 256, 256)
        rhs = cots[l][:, pl.ds(off, B), pl.ds(n0, 256)].reshape(W * B, 256)
        csend[l, u] = jnp.dot(at[l, t, 1 - c], rhs, preferred_element_type=F32).astype(BF16)
        core_copy(l, u).start()
        keep[u] = jnp.dot(at[l, t, c], rhs, preferred_element_type=F32)

    def stage_b(l, u):
        t = kind(l, u)
        p = jnp.where(t == 0, x, y)
        core_copy(l, u).wait_recv()

        def rows(o, lo, n):
            return pl.ds(pl.multiple_of(lax.rem(p + o, 4) * ROWS + lo, 16), n)

        def total(o, lo, n):
            r = rows(o, lo, n)
            return keep[u, r, :] + crecv[l, u, r, :].astype(F32)

        rsend[l, u, 0] = total(2, 0, 48).astype(BF16)
        ring_copy(l, u, 0).start()
        rsend[l, u, 1] = total(2, 48, 48).astype(BF16)
        ring_copy(l, u, 1).start()
        rsend[l, u, 2] = total(1, 48, 48).astype(BF16)
        ring_copy(l, u, 2).start()
        rsend[l, u, 3] = total(3, 0, 48).astype(BF16)
        ring_copy(l, u, 3).start()
        keep[u, rows(1, 0, 48), :] = total(1, 0, 48)
        keep[u, rows(3, 48, 48), :] = total(3, 48, 48)
        keep[u, rows(0, 0, ROWS), :] = total(0, 0, ROWS)

    def stage_c(l, u):
        t = kind(l, u)
        p = jnp.where(t == 0, x, y)
        up = pl.ds(pl.multiple_of(lax.rem(p + 1, 4) * ROWS, 16), 48)
        down = pl.ds(pl.multiple_of(lax.rem(p + 3, 4) * ROWS + 48, 16), 48)
        ring_copy(l, u, 0).wait_recv()
        rsend[l, u, 4] = (keep[u, up, :] + rrecv[l, u, 0].astype(F32)).astype(BF16)
        ring_copy(l, u, 4).start()
        ring_copy(l, u, 1).wait_recv()
        rsend[l, u, 5] = (keep[u, down, :] + rrecv[l, u, 1].astype(F32)).astype(BF16)
        ring_copy(l, u, 5).start()

    def stage_d(l, u):
        t = kind(l, u)
        p = jnp.where(t == 0, x, y)
        q = jnp.where(t == 0, y, x)
        for i in (2, 3, 4, 5):
            ring_copy(l, u, i).wait_recv()
        r0 = pl.multiple_of(p * ROWS, 16)
        half0 = keep[u, pl.ds(r0, 48), :] + rrecv[l, u, 3].astype(F32) + rrecv[l, u, 4].astype(F32)
        half1 = keep[u, pl.ds(r0 + 48, 48), :] + rrecv[l, u, 2].astype(F32) + rrecv[l, u, 5].astype(F32)
        tbuf[pl.ds(0, 2)] = half0.reshape(2, 24, 256)
        tbuf[pl.ds(2, 2)] = half1.reshape(2, 24, 256)
        for o in (2, 1, 3):
            v = tbuf[lax.rem(q + o, 4)]
            ysend[l, u, o - 1] = jnp.concatenate([v[:, :128], v[:, 128:]], axis=0).astype(BF16)
            far_copy(l, u, o).start()
        yown[u] = tbuf[q]

    def stage_e(l, u):
        for o in (1, 3, 2):
            far_copy(l, u, o).wait_recv()
        n0 = pl.multiple_of(lax.rem(u, 3) * 256, 256)
        s = yrecv[l, u, 0].astype(F32) + yrecv[l, u, 1].astype(F32) + yrecv[l, u, 2].astype(F32)
        zb[tap_of(u), :, pl.ds(n0, 256)] = yown[u] + jnp.concatenate([s[:24], s[24:]], axis=1)

    def stage_z(l):
        v = zb[...].reshape(72, C)
        pad = jnp.zeros((8, 128), F32)
        for zz in range(NZ):
            part = v[:, zz * 96 : zz * 96 + 96]
            part = jnp.concatenate([part, jnp.zeros((72, 32), F32)], axis=1)
            zf[zz] = part
            zs[l, zz] = jnp.concatenate([part, pad], axis=0).astype(BF16)
        for o in (4, 3, 5, 2, 6, 1, 7):
            z_copy(l, o).start()
        zown[l] = zf[z]

    def stage_last(l):
        for o in (1, 7, 2, 6, 3, 5, 4):
            z_copy(l, o).wait_recv()
        tot = zown[l]
        for o in range(1, NZ):
            tot = tot + zr[l, o - 1].astype(F32)[:72]
        tot = (tot * SCALE).reshape(3, 24, 128)
        gw[l] = tot[:, :, :96]


    def matmul(l, m):
        d = DIL[l]
        for n in range(3):
            acc = None
            for k in range(3):
                lhs = cots[l][pl.ds(2 * m, 2), pl.ds((2 - k) * d, B), :].reshape(2 * B, C)
                part = lax.dot_general(
                    lhs, wv[l, k, n * 256 : n * 256 + 256, :], (((1,), (1,)), ((), ())), preferred_element_type=F32
                )
                acc = part if acc is None else acc + part
            gbuf[:, n * 256 : n * 256 + 256] = acc

    def backward(l, m):
        g = gain[pl.ds(l, 1), :]
        for half in range(2):
            w = 2 * m + half
            for q in range(2):
                r = pl.ds(q * 64, 64)
                ga = gbuf[half * 128 + q * 64 : half * 128 + q * 64 + 64, :]
                inv = rstd[l, w, r, :][:, :1]
                n = xv[l, w, r, :].astype(F32) * inv
                du = ga * gp[l, w, r, :]
                sacc[l] += (du * n).reshape(8, 8, C).sum(axis=0)
                dn = du * g
                mean = jnp.mean(dn * n, axis=-1, keepdims=True)
                dx = inv * (dn - n * mean)
                if l == 1:
                    ct = c1[w, pl.ds(DIL[1] + q * 64, 64), :].astype(F32)
                    sacc[3] += ct.reshape(8, 8, C).sum(axis=0)
                    new = ct + dx
                    run[w, r, :] = new
                    nb = new.astype(BF16)
                    c0[w, pl.ds(DIL[0] + q * 64, 64), :] = nb
                    sacc[2] += nb.astype(F32).reshape(8, 8, C).sum(axis=0)
                else:
                    stage[w, r, :] = (run[w, r, :] + dx).astype(BF16)

    def out_copy(m):
        ws = pl.ds(2 * m, 2)
        return pltpu.make_async_copy(stage.at[ws], gin.at[ws], out_sem.at[m])

    bufs = (sa0, sa1, sa2, sa3)
    places = (c, x, y, z)
    counts = (2, NX, NY, NZ)
    first = (0, 1, 4, 7)

    def stat_copy(e, ax, o, sending):
        n = counts[ax]
        slot = places[ax] if sending else lax.rem(places[ax] + n - o, n)
        lo, cnt = ((0, 1), (1, 3))[e]
        to = (
            dict(to_seq=sid(y, x, 1 - c)),
            dict(to_seq=sid(y, lax.rem(x + o, NX), c)),
            dict(to_seq=sid(lax.rem(y + o, NY), x, c)),
            dict(to_z=lax.rem(z + o, NZ)),
        )[ax]
        ref = bufs[ax].at[slot, pl.ds(lo, cnt)]
        i = first[ax] + o - 1
        return rdma(ref, ref, st_s.at[e, i], st_r.at[e, i], **to)

    def stat_put(e):
        for i in ((0,), (1, 2, 3))[e]:
            v = jnp.sum(sacc[i], axis=0, keepdims=True)
            sa0[c, i] = jnp.zeros((8, 128), F32)
            for j in range(6):
                sa0[c, i, j : j + 1, :] = v[:, j * 128 : j * 128 + 128]

    def stat_send(e, ax):
        for o in range(1, counts[ax]):
            stat_copy(e, ax, o, True).start()

    def stat_recv(e, ax):
        for o in range(1, counts[ax]):
            stat_copy(e, ax, o, False).wait_recv()
        lo, cnt = ((0, 1), (1, 3))[e]
        tot = bufs[ax][0, lo : lo + cnt]
        for i in range(1, counts[ax]):
            tot = tot + bufs[ax][i, lo : lo + cnt]
        if ax < 3:
            bufs[ax + 1][places[ax + 1], lo : lo + cnt] = tot
        else:
            tot = tot * SCALE
            for i in range(cnt):
                a, b = ((0, 0), (0, 1), (1, 0), (1, 1))[lo + i]
                for j in range(6):
                    gs[a, b : b + 1, j * 128 : j * 128 + 128] = tot[i, j : j + 1, :]

    sacc[...] = jnp.zeros_like(sacc)
    ld_x[1].wait()

    @pl.loop(0, W)
    def _(w):
        forward(1, w)

    ld_c.wait()

    def grad_weight(l, before):
        @pl.loop(0, UNITS)
        def _(u):
            @pl.when(u == 3)
            def _():
                before()

            stage_a(l, u)

            @pl.when(u >= 1)
            def _():
                stage_b(l, u - 1)

            @pl.when(u >= 3)
            def _():
                stage_c(l, u - 3)

        stage_b(l, UNITS - 1)

    def drain(l, m):
        @pl.loop(0, 3)
        def _(i):
            @pl.when(m == 0)
            def _():
                stage_c(l, 6 + i)

            @pl.when(m < 3)
            def _():
                stage_d(l, 3 * m + i)

            @pl.when(m >= 1)
            def _():
                stage_e(l, 3 * m - 3 + i)

    def halo1_in():
        for h in halo1():
            h.wait_recv()
        clear_ends(1)

    def halo0_in():
        for m in range(4):
            for h in halo0(m):
                h.wait_recv()
        clear_ends(0)

    grad_weight(1, halo1_in)
    ld_w[1].wait()

    @pl.loop(0, 4)
    def _(m):
        matmul(1, m)
        backward(1, m)
        for h in halo0(m):
            h.start()
        drain(1, m)

    stage_z(1)
    ld_x[0].wait()

    @pl.loop(0, W)
    def _(w):
        forward(0, w)

    stat_put(1)
    stat_send(1, 0)
    grad_weight(0, halo0_in)
    stat_recv(1, 0)
    stat_send(1, 1)
    stage_last(1)
    ld_w[0].wait()

    @pl.loop(0, 4)
    def _(m):
        matmul(0, m)
        backward(0, m)
        out_copy(m).start()
        drain(0, m)

    stat_recv(1, 1)
    stat_send(1, 2)
    stat_put(0)
    stat_send(0, 0)
    stage_z(0)
    stat_recv(1, 2)
    stat_send(1, 3)
    stat_recv(0, 0)
    stat_send(0, 1)
    stat_recv(0, 1)
    stat_send(0, 2)
    stat_recv(0, 2)
    stat_send(0, 3)
    stage_last(0)
    stat_recv(1, 3)
    stat_recv(0, 3)

    for h in halo1():
        h.wait_send()

    @pl.loop(0, 4)
    def _(m):
        out_copy(m).wait()
        for h in halo0(m):
            h.wait_send()

    for l in range(2):

        @pl.loop(0, UNITS)
        def _(u, l=l):
            core_copy(l, u).wait_send()
            for i in range(6):
                ring_copy(l, u, i).wait_send()
            for o in range(1, 4):
                far_copy(l, u, o).wait_send()

        for o in range(1, NZ):
            z_copy(l, o).wait_send()
    for e in range(2):
        for ax in range(4):
            for o in range(1, counts[ax]):
                stat_copy(e, ax, o, True).wait_send()


def local(saved, cotangent, gain, weight):
    wt = weight.transpose(0, 2, 1, 3)
    dma = pltpu.SemaphoreType.DMA
    vm = pltpu.VMEM
    scratch = dict(
        xv=vm((2, W, B, C), BF16),
        wv=vm((2, 3, C, C), BF16),
        c0=vm((W, B + 2 * DIL[0], C), BF16),
        c1=vm((W, B + 2 * DIL[1], C), BF16),
        at=vm((2, 2, 2, 384, W * B), BF16),
        gp=vm((2, W, B, C), F32),
        rstd=vm((2, W, B, 128), F32),
        run=vm((W, B, C), F32),
        gbuf=vm((2 * B, C), F32),
        stage=vm((W, B, C), BF16),
        csend=vm((2, UNITS, 384, 256), BF16),
        crecv=vm((2, UNITS, 384, 256), BF16),
        keep=vm((UNITS, 384, 256), F32),
        rsend=vm((2, UNITS, 6, 48, 256), BF16),
        rrecv=vm((2, UNITS, 6, 48, 256), BF16),
        tbuf=vm((4, 24, 256), F32),
        ysend=vm((2, UNITS, 3, 48, 128), BF16),
        yrecv=vm((2, UNITS, 3, 48, 128), BF16),
        yown=vm((UNITS, 24, 256), F32),
        zb=vm((3, 24, C), F32),
        zs=vm((2, NZ, 80, 128), BF16),
        zf=vm((NZ, 72, 128), F32),
        zr=vm((2, NZ - 1, 80, 128), BF16),
        zown=vm((2, 72, 128), F32),
        sacc=vm((4, 8, C), F32),
        sa0=vm((2, 4, 8, 128), F32),
        sa1=vm((NX, 4, 8, 128), F32),
        sa2=vm((NY, 4, 8, 128), F32),
        sa3=vm((NZ, 4, 8, 128), F32),
        loc_sem=dma((5,)),
        out_sem=dma((4,)),
        halo_s=dma((10,)),
        halo_r=dma((10,)),
        c_s=dma((2, UNITS)),
        c_r=dma((2, UNITS)),
        r_s=dma((2, UNITS, 6)),
        r_r=dma((2, UNITS, 6)),
        y_s=dma((2, UNITS, 3)),
        y_r=dma((2, UNITS, 3)),
        z_s=dma((2, NZ - 1)),
        z_r=dma((2, NZ - 1)),
        st_s=dma((2, 14)),
        st_r=dma((2, 14)),
    )
    names = list(scratch)

    def kernel(*refs):
        named = dict(zip(names, refs[7:]))
        body(*refs[:7], **named)

    gin, gw, gs = pl.pallas_call(
        kernel,
        out_shape=(
            jax.ShapeDtypeStruct((W, B, C), BF16),
            jax.ShapeDtypeStruct((2, 3, 24, 96), F32),
            jax.ShapeDtypeStruct((2, 2, C), F32),
        ),
        in_specs=[
            pl.BlockSpec(memory_space=pl.ANY),
            pl.BlockSpec(memory_space=pl.ANY),
            pl.BlockSpec(memory_space=pltpu.VMEM),
            pl.BlockSpec(memory_space=pl.ANY),
        ],
        out_specs=(
            pl.BlockSpec(memory_space=pl.ANY),
            pl.BlockSpec(memory_space=pltpu.VMEM),
            pl.BlockSpec(memory_space=pltpu.VMEM),
        ),
        scratch_shapes=list(scratch.values()),
        compiler_params=pltpu.CompilerParams(
            collective_id=0, has_side_effects=True, vmem_limit_bytes=62 * 1024 * 1024
        ),
        cost_estimate=pl.CostEstimate(flops=14_500_000_000, bytes_accessed=13_000_000, transcendentals=1_600_000),
    )(saved, cotangent, gain, wt)
    return gin, gw.transpose(0, 2, 1, 3), gs


def solution(mesh):
    return jax.shard_map(
        local,
        mesh=mesh,
        in_specs=(P(None, "dp", "seq", None), P("dp", "seq", None), P(), P()),
        out_specs=(P("dp", "seq", None), P(None, "seq", None, "dp"), P()),
        check_vma=False,
    )
```

```python
import functools
import math

import jax
import jax.numpy as jnp
from jax import lax
from jax.experimental import pallas as pl
from jax.experimental.pallas import tpu as pltpu
from jax.sharding import PartitionSpec as P

EPS = 1e-06
F32 = jnp.float32
BF16 = jnp.bfloat16
MESH = pl.DeviceIdType.MESH

C = 768
W = 8
B = 128
DIL = (16, 32)
NX, NY, NZ = 4, 4, 8
UNITS = 9
ROWS = 96
TAPS = (1, 0, 2)
RING = (False, True)
K0 = math.sqrt(2.0 / math.pi)
K1 = 0.044715
SCALE = 1.0 / math.sqrt(64 * 4096)


def body(
    saved, cot, gain, weight, gin, gw, gs,
    xv, wv, c0, c1, at, gp, rstd, run, gbuf, stage,
    csend, crecv, keep, rsend0, rrecv0, rsend1, rrecv1, tbuf, ysend, yrecv, yown, zb, zs, zf, zr, zown,
    sacc, sa0, sa1, sa2,
    loc_sem, out_sem, halo_s, halo_r, c_s, c_r, r_s, r_r, y_s, y_r, z_s, z_r, st_s, st_r,
):
    seq = lax.axis_index("seq")
    z = lax.axis_index("dp")
    c = lax.rem(seq, 2)
    x = lax.rem(lax.div(seq, 2), NX)
    y = lax.div(seq, 2 * NX)
    cots = (c0, c1)

    def sid(yy, xx, cc):
        return (yy * NX + xx) * 2 + cc

    def rdma(src, dst, ssem, rsem, to_seq=None, to_z=None):
        where = {"seq": seq if to_seq is None else to_seq, "dp": z if to_z is None else to_z}
        return pltpu.make_async_remote_copy(
            src_ref=src, dst_ref=dst, send_sem=ssem, recv_sem=rsem, device_id=where, device_id_type=MESH
        )

    right = lax.rem(seq + 1, 32)
    left = lax.rem(seq + 31, 32)

    ld_x = [pltpu.make_async_copy(saved.at[l], xv.at[l], loc_sem.at[l]) for l in range(2)]
    ld_c = pltpu.make_async_copy(cot, c1.at[:, pl.ds(DIL[1], B), :], loc_sem.at[2])
    ld_w = [pltpu.make_async_copy(weight.at[l], wv.at[l], loc_sem.at[3 + l]) for l in range(2)]
    ld_x[1].start()
    ld_c.start()
    ld_w[1].start()
    ld_x[0].start()
    ld_w[0].start()

    def plane(o):
        return sid(lax.rem(y + o // NX, NY), lax.rem(x + o % NX, NX), c)

    bar = pltpu.get_barrier_semaphore()
    peers = [(sid(y, x, 1 - c), z), (lax.rem(seq + 2 * c + 31, 32), z)]
    peers += [(plane(o), z) for o in range(1, NX * NY)]
    peers += [(seq, lax.rem(z + o, NZ)) for o in range(1, NZ)]
    for s, zz in peers:
        pl.semaphore_signal(bar, inc=1, device_id={"seq": s, "dp": zz}, device_id_type=MESH)
    pl.semaphore_wait(bar, len(peers))

    def halo1():
        d = DIL[1]
        return (
            rdma(cot.at[:, pl.ds(0, d), :], c1.at[:, pl.ds(B + d, d), :], halo_s.at[0], halo_r.at[0], to_seq=left),
            rdma(cot.at[:, pl.ds(B - d, d), :], c1.at[:, pl.ds(0, d), :], halo_s.at[1], halo_r.at[1], to_seq=right),
        )

    def halo0(m):
        d = DIL[0]
        ws = pl.ds(2 * m, 2)
        return (
            rdma(c0.at[ws, pl.ds(d, d), :], c0.at[ws, pl.ds(B + d, d), :], halo_s.at[2 + 2 * m], halo_r.at[2 + 2 * m], to_seq=left),
            rdma(c0.at[ws, pl.ds(B, d), :], c0.at[ws, pl.ds(0, d), :], halo_s.at[3 + 2 * m], halo_r.at[3 + 2 * m], to_seq=right),
        )

    def clear_ends(l):
        d = DIL[l]
        zero = jnp.zeros((W, d, C), BF16)

        @pl.when(seq == 0)
        def _():
            cots[l][:, pl.ds(0, d), :] = zero

        @pl.when(seq == 31)
        def _():
            cots[l][:, pl.ds(B + d, d), :] = zero

    for h in halo1():
        h.start()

    def forward(l, w):
        xt = xv[l, w].astype(F32)
        g = gain[pl.ds(l, 1), :]
        inv = lax.rsqrt(jnp.mean(xt * xt, axis=-1, keepdims=True) + EPS)
        rstd[l, w] = jnp.broadcast_to(inv, (B, 128))
        u = xt * inv * g
        u2 = u * u
        t = jnp.tanh(u * (K0 + (K0 * K1) * u2))
        h = 0.5 + 0.5 * t
        act = u * h
        gp[l, w] = h + act * (1.0 - h) * (2.0 * K0 + (6.0 * K0 * K1) * u2)
        a = act.T
        cols = pl.ds(pl.multiple_of(w * B, B), B)
        for cc in range(2):
            for t_ in range(2):
                parts = []
                for dest in range(4):
                    for other in range(4):
                        yy, xx = (other, dest) if t_ == 0 else (dest, other)
                        r0 = sid(yy, xx, cc) * 24
                        parts.append(a[r0 : r0 + 24])
                at[l, t_, cc, :, cols] = jnp.concatenate(parts, axis=0).astype(BF16)

    def kind(l, u):
        return lax.rem(u + (1 - l), 2)

    def near(t, o):
        return jnp.where(t == 0, sid(y, lax.rem(x + o, NX), c), sid(lax.rem(y + o, NY), x, c))

    def far(t, o):
        return jnp.where(t == 0, sid(lax.rem(y + o, NY), x, c), sid(y, lax.rem(x + o, NX), c))

    def tap_of(u):
        return 2 - lax.rem(lax.div(u, 3) + 1, 3)

    def core_copy(l, u):
        return rdma(csend.at[l, u], crecv.at[l, u], c_s.at[l, u], c_r.at[l, u], to_seq=sid(y, x, 1 - c))

    sends, recvs = (rsend0, rsend1), (rrecv0, rrecv1)

    def ring_copy(l, u, i):
        o = (1 if i in (0, 2, 4) else 3) if RING[l] else i + 1
        return rdma(
            sends[l].at[u, i], recvs[l].at[u, i], r_s.at[l, u, i], r_r.at[l, u, i], to_seq=near(kind(l, u), o)
        )

    def far_copy(l, u, o):
        return rdma(ysend.at[l, u, o - 1], yrecv.at[l, u, o - 1], y_s.at[l, u, o - 1], y_r.at[l, u, o - 1], to_seq=far(kind(l, u), o))

    def z_copy(l, g, o):
        to = lax.rem(z + o, NZ)
        return rdma(zs.at[l, g, to], zr.at[l, g, o - 1], z_s.at[l, g, o - 1], z_r.at[l, g, o - 1], to_z=to)

    def stage_a(l, u):
        d = DIL[l]
        t = kind(l, u)
        off = pl.multiple_of(lax.rem(lax.div(u, 3) + 1, 3) * d, 16)
        n0 = pl.multiple_of(lax.rem(u, 3) * 256, 256)
        rhs = cots[l][:, pl.ds(off, B), pl.ds(n0, 256)].reshape(W * B, 256)
        csend[l, u] = jnp.dot(at[l, t, 1 - c], rhs, preferred_element_type=F32).astype(BF16)
        core_copy(l, u).start()
        keep[u] = jnp.dot(at[l, t, c], rhs, preferred_element_type=F32)

    def stage_b(l, u):
        t = kind(l, u)
        p = jnp.where(t == 0, x, y)
        core_copy(l, u).wait_recv()

        def rows(o, lo, n):
            return pl.ds(pl.multiple_of(lax.rem(p + o, 4) * ROWS + lo, 16), n)

        def total(o, lo, n):
            r = rows(o, lo, n)
            return keep[u, r, :] + crecv[l, u, r, :].astype(F32)

        if RING[l]:
            for i, o, lo in ((0, 2, 0), (1, 2, 48), (2, 1, 48), (3, 3, 0)):
                sends[l][u, i] = total(o, lo, 48).astype(BF16)
                ring_copy(l, u, i).start()
            keep[u, rows(1, 0, 48), :] = total(1, 0, 48)
            keep[u, rows(3, 48, 48), :] = total(3, 48, 48)
        else:
            for o in (2, 1, 3):
                sends[l][u, o - 1] = total(o, 0, ROWS).astype(BF16)
                ring_copy(l, u, o - 1).start()
        keep[u, rows(0, 0, ROWS), :] = total(0, 0, ROWS)

    def stage_c(l, u):
        t = kind(l, u)
        p = jnp.where(t == 0, x, y)
        up = pl.ds(pl.multiple_of(lax.rem(p + 1, 4) * ROWS, 16), 48)
        down = pl.ds(pl.multiple_of(lax.rem(p + 3, 4) * ROWS + 48, 16), 48)
        ring_copy(l, u, 0).wait_recv()
        sends[l][u, 4] = (keep[u, up, :] + recvs[l][u, 0].astype(F32)).astype(BF16)
        ring_copy(l, u, 4).start()
        ring_copy(l, u, 1).wait_recv()
        sends[l][u, 5] = (keep[u, down, :] + recvs[l][u, 1].astype(F32)).astype(BF16)
        ring_copy(l, u, 5).start()

    def stage_d(l, u):
        t = kind(l, u)
        p = jnp.where(t == 0, x, y)
        q = jnp.where(t == 0, y, x)
        for i in (2, 3, 4, 5) if RING[l] else (0, 2, 1):
            ring_copy(l, u, i).wait_recv()
        got = recvs[l]
        r0 = pl.multiple_of(p * ROWS, 16)
        if RING[l]:
            half0 = keep[u, pl.ds(r0, 48), :] + got[u, 3].astype(F32) + got[u, 4].astype(F32)
            half1 = keep[u, pl.ds(r0 + 48, 48), :] + got[u, 2].astype(F32) + got[u, 5].astype(F32)
            tbuf[pl.ds(0, 2)] = half0.reshape(2, 24, 256)
            tbuf[pl.ds(2, 2)] = half1.reshape(2, 24, 256)
        else:
            whole = keep[u, pl.ds(r0, ROWS), :] + got[u, 0].astype(F32) + got[u, 1].astype(F32) + got[u, 2].astype(F32)
            tbuf[...] = whole.reshape(4, 24, 256)
        for o in (2, 1, 3):
            v = tbuf[lax.rem(q + o, 4)]
            ysend[l, u, o - 1] = jnp.concatenate([v[:, :128], v[:, 128:]], axis=0).astype(BF16)
            far_copy(l, u, o).start()
        yown[u] = tbuf[q]

    def stage_e(l, u):
        for o in (1, 3, 2):
            far_copy(l, u, o).wait_recv()
        n0 = pl.multiple_of(lax.rem(u, 3) * 256, 256)
        s = yrecv[l, u, 0].astype(F32) + yrecv[l, u, 1].astype(F32) + yrecv[l, u, 2].astype(F32)
        zb[tap_of(u), :, pl.ds(n0, 256)] = yown[u] + jnp.concatenate([s[:24], s[24:]], axis=1)

    def stage_z(l, g):
        v = zb[TAPS[g]]
        for zz in range(NZ):
            part = jnp.concatenate([v[:, zz * 96 : zz * 96 + 96], jnp.zeros((24, 32), F32)], axis=1)
            zf[zz] = part
            zs[l, g, zz] = jnp.concatenate([part, jnp.zeros((8, 128), F32)], axis=0).astype(BF16)
        for o in (4, 3, 5, 2, 6, 1, 7):
            z_copy(l, g, o).start()
        zown[l, g] = zf[z]

    def stage_last(l, g):
        for o in (1, 7, 2, 6, 3, 5, 4):
            z_copy(l, g, o).wait_recv()
        tot = zown[l, g]
        for o in range(1, NZ):
            tot = tot + zr[l, g, o - 1].astype(F32)[:24]
        gw[l, TAPS[g]] = (tot * SCALE)[:, :96]

    def matmul(l, m):
        d = DIL[l]
        for n in range(3):
            acc = None
            for k in range(3):
                lhs = cots[l][pl.ds(2 * m, 2), pl.ds((2 - k) * d, B), :].reshape(2 * B, C)
                part = lax.dot_general(
                    lhs, wv[l, k, n * 256 : n * 256 + 256, :], (((1,), (1,)), ((), ())), preferred_element_type=F32
                )
                acc = part if acc is None else acc + part
            gbuf[:, n * 256 : n * 256 + 256] = acc

    def backward(l, m):
        g = gain[pl.ds(l, 1), :]
        for half in range(2):
            w = 2 * m + half
            for q in range(2):
                r = pl.ds(q * 64, 64)
                ga = gbuf[half * 128 + q * 64 : half * 128 + q * 64 + 64, :]
                inv = rstd[l, w, r, :][:, :1]
                n = xv[l, w, r, :].astype(F32) * inv
                du = ga * gp[l, w, r, :]
                sacc[l] += (du * n).reshape(8, 8, C).sum(axis=0)
                dn = du * g
                mean = jnp.mean(dn * n, axis=-1, keepdims=True)
                dx = inv * (dn - n * mean)
                if l == 1:
                    ct = c1[w, pl.ds(DIL[1] + q * 64, 64), :].astype(F32)
                    sacc[3] += ct.reshape(8, 8, C).sum(axis=0)
                    new = ct + dx
                    run[w, r, :] = new
                    nb = new.astype(BF16)
                    c0[w, pl.ds(DIL[0] + q * 64, 64), :] = nb
                    sacc[2] += nb.astype(F32).reshape(8, 8, C).sum(axis=0)
                else:
                    stage[w, r, :] = (run[w, r, :] + dx).astype(BF16)

    def out_copy(m):
        ws = pl.ds(2 * m, 2)
        return pltpu.make_async_copy(stage.at[ws], gin.at[ws], out_sem.at[m])

    bufs = (sa0, sa1, sa2)
    places = (c, y * NX + x, z)
    counts = (2, NX * NY, NZ)
    first = (0, 1, NX * NY)

    def stat_copy(e, ax, o, sending):
        lo, cnt = ((0, 1), (1, 3))[e]
        if ax == 0:
            to, back = dict(to_seq=sid(y, x, 1 - c)), 1 - c
        elif ax == 1:
            to = dict(to_seq=plane(o))
            back = lax.rem(y + NY - o // NX, NY) * NX + lax.rem(x + NX - o % NX, NX)
        else:
            to, back = dict(to_z=lax.rem(z + o, NZ)), lax.rem(z + NZ - o, NZ)
        ref = bufs[ax].at[places[ax] if sending else back, pl.ds(lo, cnt)]
        i = first[ax] + o - 1
        return rdma(ref, ref, st_s.at[e, i], st_r.at[e, i], **to)

    def stat_put(e):
        for i in ((0,), (1, 2, 3))[e]:
            v = jnp.sum(sacc[i], axis=0, keepdims=True)
            sa0[c, i] = jnp.zeros((8, 128), F32)
            for j in range(6):
                sa0[c, i, j : j + 1, :] = v[:, j * 128 : j * 128 + 128]

    def stat_send(e, ax):
        for o in range(1, counts[ax]):
            stat_copy(e, ax, o, True).start()

    def stat_recv(e, ax):
        for o in range(1, counts[ax]):
            stat_copy(e, ax, o, False).wait_recv()
        lo, cnt = ((0, 1), (1, 3))[e]
        tot = bufs[ax][0, lo : lo + cnt]
        for i in range(1, counts[ax]):
            tot = tot + bufs[ax][i, lo : lo + cnt]
        if ax < 2:
            bufs[ax + 1][places[ax + 1], lo : lo + cnt] = tot
        else:
            tot = tot * SCALE
            for i in range(cnt):
                a, b = ((0, 0), (0, 1), (1, 0), (1, 1))[lo + i]
                for j in range(6):
                    gs[a, b : b + 1, j * 128 : j * 128 + 128] = tot[i, j : j + 1, :]

    sacc[...] = jnp.zeros_like(sacc)
    ld_x[1].wait()

    @pl.loop(0, W)
    def _(w):
        forward(1, w)

    ld_x[0].wait()

    @pl.loop(0, W)
    def _(w):
        forward(0, w)

    ld_c.wait()

    @pl.loop(0, 3)
    def _(u):
        stage_a(1, u)

    for h in halo1():
        h.wait_recv()
    clear_ends(1)

    @pl.loop(3, UNITS)
    def _(u):
        stage_a(1, u)
        stage_b(1, u - 3)

    ld_w[1].wait()

    @pl.loop(0, 4)
    def _(m):
        matmul(1, m)
        backward(1, m)
        for h in halo0(m):
            h.start()

        @pl.loop(0, 3)
        def _(i):
            @pl.when(m == 0)
            def _():
                stage_b(1, 6 + i)

            if RING[1]:

                @pl.when(m < 3)
                def _():
                    stage_c(1, 3 * m + i)

            @pl.when(m >= 2)
            def _():
                stage_d(1, 3 * (m - 2) + i)

    stat_put(1)
    stat_send(1, 0)

    @pl.loop(0, 3)
    def _(u):
        stage_a(0, u)
        stage_d(1, 6 + u)
        stage_e(1, u)

    stat_recv(1, 0)
    stat_send(1, 1)
    for m in range(4):
        for h in halo0(m):
            h.wait_recv()
    clear_ends(0)

    @pl.loop(3, UNITS)
    def _(u):
        stage_a(0, u)
        stage_b(0, u - 3)
        stage_e(1, u)

    for g in range(3):
        stage_z(1, g)
    ld_w[0].wait()

    @pl.loop(0, 4)
    def _(m):
        matmul(0, m)
        backward(0, m)
        out_copy(m).start()

        @pl.loop(0, 3)
        def _(i):
            @pl.when(m == 0)
            def _():
                stage_b(0, 6 + i)

            if RING[0]:

                @pl.when(m < 3)
                def _():
                    stage_c(0, 3 * m + i)

                @pl.when(m >= 2)
                def _():
                    stage_d(0, 3 * (m - 2) + i)

            else:

                @pl.when(m >= 2)
                def _():
                    stage_d(0, 3 * (m - 2) + i)

    stat_put(0)
    stat_send(0, 0)
    stat_recv(1, 1)
    stat_send(1, 2)
    stat_recv(0, 0)
    stat_send(0, 1)
    for g in range(3):
        stage_last(1, g)

    @pl.loop(6, UNITS)
    def _(u):
        stage_d(0, u)

    @pl.loop(0, 3)
    def _(u):
        stage_e(0, u)

    stage_z(0, 0)

    @pl.loop(3, 6)
    def _(u):
        stage_e(0, u)

    stage_z(0, 1)
    stat_recv(0, 1)
    stat_send(0, 2)

    @pl.loop(6, UNITS)
    def _(u):
        stage_e(0, u)

    stage_z(0, 2)
    stat_recv(1, 2)
    stage_last(0, 0)
    stage_last(0, 1)
    stat_recv(0, 2)
    stage_last(0, 2)

    for h in halo1():
        h.wait_send()

    @pl.loop(0, 4)
    def _(m):
        out_copy(m).wait()
        for h in halo0(m):
            h.wait_send()

    for l in range(2):

        @pl.loop(0, UNITS)
        def _(u, l=l):
            core_copy(l, u).wait_send()
            for i in range(6 if RING[l] else 3):
                ring_copy(l, u, i).wait_send()
            for o in range(1, 4):
                far_copy(l, u, o).wait_send()

        for g in range(3):
            for o in range(1, NZ):
                z_copy(l, g, o).wait_send()
    for e in range(2):
        for ax in range(3):
            for o in range(1, counts[ax]):
                stat_copy(e, ax, o, True).wait_send()


def last_copy(a, b, c, a_out, b_out, c_out, sem):
    copies = [pltpu.make_async_copy(a.at[w], a_out.at[w], sem.at[w]) for w in range(W)]
    copies += [pltpu.make_async_copy(b, b_out, sem.at[W]), pltpu.make_async_copy(c, c_out, sem.at[W + 1])]
    for copy in copies:
        copy.start()
    for copy in copies:
        copy.wait()


def local(saved, cotangent, gain, weight):
    wt = weight.transpose(0, 2, 1, 3)
    dma = pltpu.SemaphoreType.DMA

    def part(l):
        return (6, 48) if RING[l] else (3, 96)

    vm = pltpu.VMEM
    scratch = dict(
        xv=vm((2, W, B, C), BF16),
        wv=vm((2, 3, C, C), BF16),
        c0=vm((W, B + 2 * DIL[0], C), BF16),
        c1=vm((W, B + 2 * DIL[1], C), BF16),
        at=vm((2, 2, 2, 384, W * B), BF16),
        gp=vm((2, W, B, C), F32),
        rstd=vm((2, W, B, 128), F32),
        run=vm((W, B, C), F32),
        gbuf=vm((2 * B, C), F32),
        stage=vm((W, B, C), BF16),
        csend=vm((2, UNITS, 384, 256), BF16),
        crecv=vm((2, UNITS, 384, 256), BF16),
        keep=vm((UNITS, 384, 256), F32),
        rsend0=vm((UNITS, *part(0), 256), BF16),
        rrecv0=vm((UNITS, *part(0), 256), BF16),
        rsend1=vm((UNITS, *part(1), 256), BF16),
        rrecv1=vm((UNITS, *part(1), 256), BF16),
        tbuf=vm((4, 24, 256), F32),
        ysend=vm((2, UNITS, 3, 48, 128), BF16),
        yrecv=vm((2, UNITS, 3, 48, 128), BF16),
        yown=vm((UNITS, 24, 256), F32),
        zb=vm((3, 24, C), F32),
        zs=vm((2, 3, NZ, 32, 128), BF16),
        zf=vm((NZ, 24, 128), F32),
        zr=vm((2, 3, NZ - 1, 32, 128), BF16),
        zown=vm((2, 3, 24, 128), F32),
        sacc=vm((4, 8, C), F32),
        sa0=vm((2, 4, 8, 128), F32),
        sa1=vm((NX * NY, 4, 8, 128), F32),
        sa2=vm((NZ, 4, 8, 128), F32),
        loc_sem=dma((5,)),
        out_sem=dma((4,)),
        halo_s=dma((10,)),
        halo_r=dma((10,)),
        c_s=dma((2, UNITS)),
        c_r=dma((2, UNITS)),
        r_s=dma((2, UNITS, 6)),
        r_r=dma((2, UNITS, 6)),
        y_s=dma((2, UNITS, 3)),
        y_r=dma((2, UNITS, 3)),
        z_s=dma((2, 3, NZ - 1)),
        z_r=dma((2, 3, NZ - 1)),
        st_s=dma((2, 23)),
        st_r=dma((2, 23)),
    )
    names = list(scratch)

    def kernel(*refs):
        named = dict(zip(names, refs[7:]))
        body(*refs[:7], **named)

    gin, gw, gs = pl.pallas_call(
        kernel,
        out_shape=(
            jax.ShapeDtypeStruct((W, B, C), BF16),
            jax.ShapeDtypeStruct((2, 3, 24, 96), F32),
            jax.ShapeDtypeStruct((2, 2, C), F32),
        ),
        in_specs=[
            pl.BlockSpec(memory_space=pl.ANY),
            pl.BlockSpec(memory_space=pl.ANY),
            pl.BlockSpec(memory_space=pltpu.VMEM),
            pl.BlockSpec(memory_space=pl.ANY),
        ],
        out_specs=(
            pl.BlockSpec(memory_space=pl.ANY),
            pl.BlockSpec(memory_space=pltpu.VMEM),
            pl.BlockSpec(memory_space=pltpu.VMEM),
        ),
        scratch_shapes=list(scratch.values()),
        compiler_params=pltpu.CompilerParams(
            collective_id=0, has_side_effects=True, vmem_limit_bytes=62 * 1024 * 1024
        ),
        cost_estimate=pl.CostEstimate(flops=14_500_000_000, bytes_accessed=13_000_000, transcendentals=1_600_000),
    )(saved, cotangent, gain, wt)
    gin, gw, gs = pl.pallas_call(
        last_copy,
        out_shape=tuple(jax.ShapeDtypeStruct(v.shape, v.dtype) for v in (gin, gw, gs)),
        in_specs=[pl.BlockSpec(memory_space=pl.ANY)] * 3,
        out_specs=(pl.BlockSpec(memory_space=pl.ANY),) * 3,
        scratch_shapes=[dma((W + 2,))],
        compiler_params=pltpu.CompilerParams(has_side_effects=True),
    )(gin, gw, gs)
    return gin, gw.transpose(0, 2, 1, 3), gs


def solution(mesh):
    return jax.shard_map(
        local,
        mesh=mesh,
        in_specs=(P(None, "dp", "seq", None), P("dp", "seq", None), P(), P()),
        out_specs=(P("dp", "seq", None), P(None, "seq", None, "dp"), P()),
        check_vma=False,
    )
```

```python
import functools
import math

import jax
import jax.numpy as jnp
from jax import lax
from jax.experimental import pallas as pl
from jax.experimental.pallas import tpu as pltpu
from jax.sharding import PartitionSpec as P

EPS = 1e-06
F32 = jnp.float32
BF16 = jnp.bfloat16
MESH = pl.DeviceIdType.MESH

C = 768
W = 8
B = 128
DIL = (16, 32)
NX, NY, NZ = 4, 4, 8
UNITS = 9
ROWS = 96
TAPS = (1, 0, 2)
RING = (False, True)
K0 = math.sqrt(2.0 / math.pi)
K1 = 0.044715
SCALE = 1.0 / math.sqrt(64 * 4096)


def body(
    saved, cot, gain, weight, gin, gw, gs,
    xv, wv, c0, c1, at0, at1, gp, rstd, run, gbuf, stage,
    csend, crecv, keep, rsend0, rrecv0, rsend1, rrecv1, tbuf, ysend, yrecv, yown, zb, zs, zf, zr, zown,
    sacc, sa0, sa1, sa2,
    x1_sem, loc_sem, out_sem, halo_s, halo_r, c_s, c_r, r_s, r_r, y_s, y_r, z_s, z_r, st_s, st_r,
):
    seq = lax.axis_index("seq")
    z = lax.axis_index("dp")
    c = lax.rem(seq, 2)
    x = lax.rem(lax.div(seq, 2), NX)
    y = lax.div(seq, 2 * NX)
    cots = (c0, c1)
    ats = (at0, at1)

    def sid(yy, xx, cc):
        return (yy * NX + xx) * 2 + cc

    def rdma(src, dst, ssem, rsem, to_seq=None, to_z=None):
        where = {"seq": seq if to_seq is None else to_seq, "dp": z if to_z is None else to_z}
        return pltpu.make_async_remote_copy(
            src_ref=src, dst_ref=dst, send_sem=ssem, recv_sem=rsem, device_id=where, device_id_type=MESH
        )

    right = lax.rem(seq + 1, 32)
    left = lax.rem(seq + 31, 32)

    ld_x1 = [pltpu.make_async_copy(saved.at[1, w], xv.at[1, w], x1_sem.at[w]) for w in range(W)]
    ld_x0 = pltpu.make_async_copy(saved.at[0], xv.at[0], loc_sem.at[0])
    ld_c = pltpu.make_async_copy(cot, c1.at[:, pl.ds(DIL[1], B), :], loc_sem.at[2])
    ld_w = [pltpu.make_async_copy(weight.at[l], wv.at[l], loc_sem.at[3 + l]) for l in range(2)]
    for ld in ld_x1:
        ld.start()
    ld_c.start()

    def plane(o):
        return sid(lax.rem(y + o // NX, NY), lax.rem(x + o % NX, NX), c)

    bar = pltpu.get_barrier_semaphore()
    peers = [(sid(y, x, 1 - c), z), (lax.rem(seq + 2 * c + 31, 32), z)]
    peers += [(plane(o), z) for o in range(1, NX * NY)]
    peers += [(seq, lax.rem(z + o, NZ)) for o in range(1, NZ)]
    for s, zz in peers:
        pl.semaphore_signal(bar, inc=1, device_id={"seq": s, "dp": zz}, device_id_type=MESH)
    pl.semaphore_wait(bar, len(peers))

    def halo1():
        d = DIL[1]
        return (
            rdma(cot.at[:, pl.ds(0, d), :], c1.at[:, pl.ds(B + d, d), :], halo_s.at[0], halo_r.at[0], to_seq=left),
            rdma(cot.at[:, pl.ds(B - d, d), :], c1.at[:, pl.ds(0, d), :], halo_s.at[1], halo_r.at[1], to_seq=right),
        )

    def halo0(m):
        d = DIL[0]
        ws = pl.ds(2 * m, 2)
        return (
            rdma(c0.at[ws, pl.ds(d, d), :], c0.at[ws, pl.ds(B + d, d), :], halo_s.at[2 + 2 * m], halo_r.at[2 + 2 * m], to_seq=left),
            rdma(c0.at[ws, pl.ds(B, d), :], c0.at[ws, pl.ds(0, d), :], halo_s.at[3 + 2 * m], halo_r.at[3 + 2 * m], to_seq=right),
        )

    def clear_ends(l):
        d = DIL[l]
        zero = jnp.zeros((W, d, C), BF16)

        @pl.when(seq == 0)
        def _():
            cots[l][:, pl.ds(0, d), :] = zero

        @pl.when(seq == 31)
        def _():
            cots[l][:, pl.ds(B + d, d), :] = zero

    for h in halo1():
        h.start()

    def forward(l, w):
        xt = xv[l, w].astype(F32)
        g = gain[pl.ds(l, 1), :]
        inv = lax.rsqrt(jnp.mean(xt * xt, axis=-1, keepdims=True) + EPS)
        rstd[l, w] = jnp.broadcast_to(inv, (B, 128))
        u = xt * inv * g
        u2 = u * u
        t = jnp.tanh(u * (K0 + (K0 * K1) * u2))
        h = 0.5 + 0.5 * t
        act = u * h
        gp[l, w] = h + act * (1.0 - h) * (2.0 * K0 + (6.0 * K0 * K1) * u2)
        a = act.T
        cols = pl.ds(pl.multiple_of(w * B, B), B)
        for cc in range(2):
            for t_ in range(2):
                parts = []
                for dest in range(4):
                    for other in range(4):
                        yy, xx = (other, dest) if t_ == 0 else (dest, other)
                        r0 = sid(yy, xx, cc) * 24
                        parts.append(a[r0 : r0 + 24])
                ats[l][t_, cc, :, cols] = jnp.concatenate(parts, axis=0).astype(BF16)

    def kind(l, u):
        return lax.rem(u + (1 - l), 2)

    def near(t, o):
        return jnp.where(t == 0, sid(y, lax.rem(x + o, NX), c), sid(lax.rem(y + o, NY), x, c))

    def far(t, o):
        return jnp.where(t == 0, sid(lax.rem(y + o, NY), x, c), sid(y, lax.rem(x + o, NX), c))

    def tap_of(u):
        return 2 - lax.rem(lax.div(u, 3) + 1, 3)

    def core_copy(l, u):
        return rdma(csend.at[l, u], crecv.at[l, u], c_s.at[l, u], c_r.at[l, u], to_seq=sid(y, x, 1 - c))

    sends, recvs = (rsend0, rsend1), (rrecv0, rrecv1)

    def ring_copy(l, u, i):
        o = (1 if i in (0, 2, 4) else 3) if RING[l] else i + 1
        return rdma(
            sends[l].at[u, i], recvs[l].at[u, i], r_s.at[l, u, i], r_r.at[l, u, i], to_seq=near(kind(l, u), o)
        )

    def far_copy(l, u, o):
        return rdma(ysend.at[l, u, o - 1], yrecv.at[l, u, o - 1], y_s.at[l, u, o - 1], y_r.at[l, u, o - 1], to_seq=far(kind(l, u), o))

    def z_copy(l, g, o):
        to = lax.rem(z + o, NZ)
        return rdma(zs.at[l, g, to], zr.at[l, g, o - 1], z_s.at[l, g, o - 1], z_r.at[l, g, o - 1], to_z=to)

    def stage_a(l, u, beside=None):
        d = DIL[l]
        t = kind(l, u)
        off = pl.multiple_of(lax.rem(lax.div(u, 3) + 1, 3) * d, 16)
        n0 = pl.multiple_of(lax.rem(u, 3) * 256, 256)
        rhs = cots[l][:, pl.ds(off, B), pl.ds(n0, 256)].reshape(W * B, 256)
        csend[l, u] = jnp.dot(ats[l][t, 1 - c], rhs, preferred_element_type=F32).astype(BF16)
        keep[l, u] = jnp.dot(ats[l][t, c], rhs, preferred_element_type=F32)
        if beside is not None:
            beside()
        core_copy(l, u).start()

    def stage_b(l, u):
        t = kind(l, u)
        p = jnp.where(t == 0, x, y)
        core_copy(l, u).wait_recv()

        def rows(o, lo, n):
            return pl.ds(pl.multiple_of(lax.rem(p + o, 4) * ROWS + lo, 16), n)

        def total(o, lo, n):
            r = rows(o, lo, n)
            return keep[l, u, r, :] + crecv[l, u, r, :].astype(F32)

        if RING[l]:
            for i, o, lo in ((0, 2, 0), (1, 2, 48), (2, 1, 48), (3, 3, 0)):
                sends[l][u, i] = total(o, lo, 48).astype(BF16)
                ring_copy(l, u, i).start()
            keep[l, u, rows(1, 0, 48), :] = total(1, 0, 48)
            keep[l, u, rows(3, 48, 48), :] = total(3, 48, 48)
        else:
            for o in (2, 1, 3):
                sends[l][u, o - 1] = total(o, 0, ROWS).astype(BF16)
                ring_copy(l, u, o - 1).start()
        keep[l, u, rows(0, 0, ROWS), :] = total(0, 0, ROWS)

    def stage_c(l, u):
        t = kind(l, u)
        p = jnp.where(t == 0, x, y)
        up = pl.ds(pl.multiple_of(lax.rem(p + 1, 4) * ROWS, 16), 48)
        down = pl.ds(pl.multiple_of(lax.rem(p + 3, 4) * ROWS + 48, 16), 48)
        ring_copy(l, u, 0).wait_recv()
        sends[l][u, 4] = (keep[l, u, up, :] + recvs[l][u, 0].astype(F32)).astype(BF16)
        ring_copy(l, u, 4).start()
        ring_copy(l, u, 1).wait_recv()
        sends[l][u, 5] = (keep[l, u, down, :] + recvs[l][u, 1].astype(F32)).astype(BF16)
        ring_copy(l, u, 5).start()

    def stage_d(l, u):
        t = kind(l, u)
        p = jnp.where(t == 0, x, y)
        q = jnp.where(t == 0, y, x)
        for i in (2, 3, 4, 5) if RING[l] else (0, 2, 1):
            ring_copy(l, u, i).wait_recv()
        got = recvs[l]
        r0 = pl.multiple_of(p * ROWS, 16)
        if RING[l]:
            half0 = keep[l, u, pl.ds(r0, 48), :] + got[u, 3].astype(F32) + got[u, 4].astype(F32)
            half1 = keep[l, u, pl.ds(r0 + 48, 48), :] + got[u, 2].astype(F32) + got[u, 5].astype(F32)
            tbuf[pl.ds(0, 2)] = half0.reshape(2, 24, 256)
            tbuf[pl.ds(2, 2)] = half1.reshape(2, 24, 256)
        else:
            whole = keep[l, u, pl.ds(r0, ROWS), :] + got[u, 0].astype(F32) + got[u, 1].astype(F32) + got[u, 2].astype(F32)
            tbuf[...] = whole.reshape(4, 24, 256)
        for o in (2, 1, 3):
            v = tbuf[lax.rem(q + o, 4)]
            ysend[l, u, o - 1] = jnp.concatenate([v[:, :128], v[:, 128:]], axis=0).astype(BF16)
            far_copy(l, u, o).start()
        yown[u] = tbuf[q]

    def stage_e(l, u):
        for o in (1, 3, 2):
            far_copy(l, u, o).wait_recv()
        n0 = pl.multiple_of(lax.rem(u, 3) * 256, 256)
        s = yrecv[l, u, 0].astype(F32) + yrecv[l, u, 1].astype(F32) + yrecv[l, u, 2].astype(F32)
        zb[tap_of(u), :, pl.ds(n0, 256)] = yown[u] + jnp.concatenate([s[:24], s[24:]], axis=1)

    def stage_z(l, g):
        v = zb[TAPS[g]]
        for zz in range(NZ):
            part = jnp.concatenate([v[:, zz * 96 : zz * 96 + 96], jnp.zeros((24, 32), F32)], axis=1)
            zf[zz] = part
            zs[l, g, zz] = jnp.concatenate([part, jnp.zeros((8, 128), F32)], axis=0).astype(BF16)
        for o in (4, 3, 5, 2, 6, 1, 7):
            z_copy(l, g, o).start()
        zown[l, g] = zf[z]

    def stage_last(l, g):
        for o in (1, 7, 2, 6, 3, 5, 4):
            z_copy(l, g, o).wait_recv()
        tot = zown[l, g]
        for o in range(1, NZ):
            tot = tot + zr[l, g, o - 1].astype(F32)[:24]
        gw[l, TAPS[g]] = (tot * SCALE)[:, :96]

    def matmul(l, m):
        d = DIL[l]
        for n in range(3):
            acc = None
            for k in range(3):
                lhs = cots[l][pl.ds(2 * m, 2), pl.ds((2 - k) * d, B), :].reshape(2 * B, C)
                part = lax.dot_general(
                    lhs, wv[l, k, n * 256 : n * 256 + 256, :], (((1,), (1,)), ((), ())), preferred_element_type=F32
                )
                acc = part if acc is None else acc + part
            gbuf[:, n * 256 : n * 256 + 256] = acc

    def backward(l, m):
        g = gain[pl.ds(l, 1), :]
        for half in range(2):
            w = 2 * m + half
            for q in range(2):
                r = pl.ds(q * 64, 64)
                ga = gbuf[half * 128 + q * 64 : half * 128 + q * 64 + 64, :]
                inv = rstd[l, w, r, :][:, :1]
                n = xv[l, w, r, :].astype(F32) * inv
                du = ga * gp[l, w, r, :]
                sacc[l] += (du * n).reshape(8, 8, C).sum(axis=0)
                dn = du * g
                mean = jnp.mean(dn * n, axis=-1, keepdims=True)
                dx = inv * (dn - n * mean)
                if l == 1:
                    ct = c1[w, pl.ds(DIL[1] + q * 64, 64), :].astype(F32)
                    sacc[3] += ct.reshape(8, 8, C).sum(axis=0)
                    new = ct + dx
                    run[w, r, :] = new
                    nb = new.astype(BF16)
                    c0[w, pl.ds(DIL[0] + q * 64, 64), :] = nb
                    sacc[2] += nb.astype(F32).reshape(8, 8, C).sum(axis=0)
                else:
                    stage[w, r, :] = (run[w, r, :] + dx).astype(BF16)

    def out_copy(m):
        ws = pl.ds(2 * m, 2)
        return pltpu.make_async_copy(stage.at[ws], gin.at[ws], out_sem.at[m])

    bufs = (sa0, sa1, sa2)
    places = (c, y * NX + x, z)
    counts = (2, NX * NY, NZ)
    first = (0, 1, NX * NY)

    def stat_copy(e, ax, o, sending):
        lo, cnt = ((0, 1), (1, 3))[e]
        if ax == 0:
            to, back = dict(to_seq=sid(y, x, 1 - c)), 1 - c
        elif ax == 1:
            to = dict(to_seq=plane(o))
            back = lax.rem(y + NY - o // NX, NY) * NX + lax.rem(x + NX - o % NX, NX)
        else:
            to, back = dict(to_z=lax.rem(z + o, NZ)), lax.rem(z + NZ - o, NZ)
        ref = bufs[ax].at[places[ax] if sending else back, pl.ds(lo, cnt)]
        i = first[ax] + o - 1
        return rdma(ref, ref, st_s.at[e, i], st_r.at[e, i], **to)

    def stat_put(e):
        for i in ((0,), (1, 2, 3))[e]:
            v = jnp.sum(sacc[i], axis=0, keepdims=True)
            sa0[c, i] = jnp.zeros((8, 128), F32)
            for j in range(6):
                sa0[c, i, j : j + 1, :] = v[:, j * 128 : j * 128 + 128]

    def stat_send(e, ax):
        for o in range(1, counts[ax]):
            stat_copy(e, ax, o, True).start()

    def stat_recv(e, ax):
        for o in range(1, counts[ax]):
            stat_copy(e, ax, o, False).wait_recv()
        lo, cnt = ((0, 1), (1, 3))[e]
        tot = bufs[ax][0, lo : lo + cnt]
        for i in range(1, counts[ax]):
            tot = tot + bufs[ax][i, lo : lo + cnt]
        if ax < 2:
            bufs[ax + 1][places[ax + 1], lo : lo + cnt] = tot
        else:
            tot = tot * SCALE
            for i in range(cnt):
                a, b = ((0, 0), (0, 1), (1, 0), (1, 1))[lo + i]
                for j in range(6):
                    gs[a, b : b + 1, j * 128 : j * 128 + 128] = tot[i, j : j + 1, :]

    sacc[...] = jnp.zeros_like(sacc)
    ld_x0.start()

    @pl.loop(0, W)
    def _(w):
        pltpu.make_async_copy(saved.at[1, w], xv.at[1, w], x1_sem.at[w]).wait()
        forward(1, w)

    ld_w[1].start()
    ld_w[0].start()
    ld_c.wait()
    ld_x0.wait()

    @pl.loop(0, 3)
    def _(u):
        stage_a(1, u, lambda: forward(0, u))

    for h in halo1():
        h.wait_recv()
    clear_ends(1)

    @pl.loop(3, 8)
    def _(u):
        stage_a(1, u, lambda: forward(0, u))
        stage_b(1, u - 3)

    stage_a(1, 8)
    stage_b(1, 5)
    ld_w[1].wait()

    @pl.loop(0, 4)
    def _(m):
        matmul(1, m)
        backward(1, m)
        for h in halo0(m):
            h.start()

        @pl.loop(0, 3)
        def _(i):
            @pl.when(m == 0)
            def _():
                stage_b(1, 6 + i)

            if RING[1]:

                @pl.when(m >= 1)
                def _():
                    stage_c(1, 3 * m - 3 + i)

    stat_put(1)
    stat_send(1, 0)

    @pl.loop(0, 3)
    def _(u):
        stage_a(0, u)
        stage_d(1, u)

    stat_recv(1, 0)
    stat_send(1, 1)
    for m in range(4):
        for h in halo0(m):
            h.wait_recv()
    clear_ends(0)

    @pl.loop(3, UNITS)
    def _(u):
        stage_a(0, u)
        stage_b(0, u - 3)
        stage_d(1, u)

    ld_w[0].wait()

    @pl.loop(0, 4)
    def _(m):
        matmul(0, m)
        backward(0, m)
        out_copy(m).start()

        @pl.loop(0, 3)
        def _(i):
            @pl.when(m == 0)
            def _():
                stage_b(0, 6 + i)

            if RING[0]:

                @pl.when(m < 3)
                def _():
                    stage_c(0, 3 * m + i)

            @pl.when(m == 3)
            def _():
                stage_d(0, i)

            @pl.when(m >= 1)
            def _():
                stage_e(1, 3 * m - 3 + i)

    stat_put(0)
    stat_send(0, 0)
    stat_recv(1, 1)
    stat_send(1, 2)
    stat_recv(0, 0)
    stat_send(0, 1)
    for g in range(3):
        stage_z(1, g)

    @pl.loop(3, UNITS)
    def _(u):
        stage_d(0, u)

    stat_recv(0, 1)
    stat_send(0, 2)
    for g in range(3):

        @pl.loop(3 * g, 3 * g + 3)
        def _(u):
            stage_e(0, u)

        stage_z(0, g)
        if g == 0:
            for k in range(3):
                stage_last(1, k)
            stat_recv(1, 2)

    stat_recv(0, 2)
    for g in range(3):
        stage_last(0, g)

    for h in halo1():
        h.wait_send()

    @pl.loop(0, 4)
    def _(m):
        out_copy(m).wait()
        for h in halo0(m):
            h.wait_send()

    for l in range(2):

        @pl.loop(0, UNITS)
        def _(u, l=l):
            core_copy(l, u).wait_send()
            for i in range(6 if RING[l] else 3):
                ring_copy(l, u, i).wait_send()
            for o in range(1, 4):
                far_copy(l, u, o).wait_send()

        for g in range(3):
            for o in range(1, NZ):
                z_copy(l, g, o).wait_send()
    for e in range(2):
        for ax in range(3):
            for o in range(1, counts[ax]):
                stat_copy(e, ax, o, True).wait_send()


def last_copy(a, b, c, a_out, b_out, c_out, at, sem):
    into = [pltpu.make_async_copy(a.at[w], at.at[w], sem.at[w]) for w in range(W)]
    out = [pltpu.make_async_copy(at.at[w], a_out.at[w], sem.at[W + w]) for w in range(W)]
    for copy in into:
        copy.start()
    b_out[...] = b[...]
    c_out[...] = c[...]
    for first, second in zip(into, out):
        first.wait()
        second.start()
    for copy in out:
        copy.wait()


def local(saved, cotangent, gain, weight):
    wt = weight.transpose(0, 2, 1, 3)
    dma = pltpu.SemaphoreType.DMA

    def part(l):
        return (6, 48) if RING[l] else (3, 96)

    vm = pltpu.VMEM
    scratch = dict(
        xv=vm((2, W, B, C), BF16),
        wv=vm((2, 3, C, C), BF16),
        c0=vm((W, B + 2 * DIL[0], C), BF16),
        c1=vm((W, B + 2 * DIL[1], C), BF16),
        at0=vm((2, 2, 384, W * B), BF16),
        at1=vm((2, 2, 384, W * B), BF16),
        gp=vm((2, W, B, C), F32),
        rstd=vm((2, W, B, 128), F32),
        run=vm((W, B, C), F32),
        gbuf=vm((2 * B, C), F32),
        stage=vm((W, B, C), BF16),
        csend=vm((2, UNITS, 384, 256), BF16),
        crecv=vm((2, UNITS, 384, 256), BF16),
        keep=vm((2, UNITS, 384, 256), F32),
        rsend0=vm((UNITS, *part(0), 256), BF16),
        rrecv0=vm((UNITS, *part(0), 256), BF16),
        rsend1=vm((UNITS, *part(1), 256), BF16),
        rrecv1=vm((UNITS, *part(1), 256), BF16),
        tbuf=vm((4, 24, 256), F32),
        ysend=vm((2, UNITS, 3, 48, 128), BF16),
        yrecv=vm((2, UNITS, 3, 48, 128), BF16),
        yown=vm((UNITS, 24, 256), F32),
        zb=vm((3, 24, C), F32),
        zs=vm((2, 3, NZ, 32, 128), BF16),
        zf=vm((NZ, 24, 128), F32),
        zr=vm((2, 3, NZ - 1, 32, 128), BF16),
        zown=vm((2, 3, 24, 128), F32),
        sacc=vm((4, 8, C), F32),
        sa0=vm((2, 4, 8, 128), F32),
        sa1=vm((NX * NY, 4, 8, 128), F32),
        sa2=vm((NZ, 4, 8, 128), F32),
        x1_sem=dma((W,)),
        loc_sem=dma((5,)),
        out_sem=dma((4,)),
        halo_s=dma((10,)),
        halo_r=dma((10,)),
        c_s=dma((2, UNITS)),
        c_r=dma((2, UNITS)),
        r_s=dma((2, UNITS, 6)),
        r_r=dma((2, UNITS, 6)),
        y_s=dma((2, UNITS, 3)),
        y_r=dma((2, UNITS, 3)),
        z_s=dma((2, 3, NZ - 1)),
        z_r=dma((2, 3, NZ - 1)),
        st_s=dma((2, 23)),
        st_r=dma((2, 23)),
    )
    names = list(scratch)

    def kernel(*refs):
        named = dict(zip(names, refs[7:]))
        body(*refs[:7], **named)

    gin, gw, gs = pl.pallas_call(
        kernel,
        out_shape=(
            jax.ShapeDtypeStruct((W, B, C), BF16),
            jax.ShapeDtypeStruct((2, 3, 24, 96), F32),
            jax.ShapeDtypeStruct((2, 2, C), F32),
        ),
        in_specs=[
            pl.BlockSpec(memory_space=pl.ANY),
            pl.BlockSpec(memory_space=pl.ANY),
            pl.BlockSpec(memory_space=pltpu.VMEM),
            pl.BlockSpec(memory_space=pl.ANY),
        ],
        out_specs=(
            pl.BlockSpec(memory_space=pl.ANY),
            pl.BlockSpec(memory_space=pltpu.VMEM),
            pl.BlockSpec(memory_space=pltpu.VMEM),
        ),
        scratch_shapes=list(scratch.values()),
        compiler_params=pltpu.CompilerParams(
            collective_id=0, has_side_effects=True, vmem_limit_bytes=62 * 1024 * 1024
        ),
        cost_estimate=pl.CostEstimate(flops=14_500_000_000, bytes_accessed=13_000_000, transcendentals=1_600_000),
    )(saved, cotangent, gain, wt)
    gin, gw, gs = pl.pallas_call(
        last_copy,
        out_shape=tuple(jax.ShapeDtypeStruct(v.shape, v.dtype) for v in (gin, gw, gs)),
        in_specs=[pl.BlockSpec(memory_space=pl.ANY)] + [pl.BlockSpec(memory_space=vm)] * 2,
        out_specs=(pl.BlockSpec(memory_space=pl.ANY),) + (pl.BlockSpec(memory_space=vm),) * 2,
        scratch_shapes=[vm((W, B, C), BF16), dma((2 * W,))],
        compiler_params=pltpu.CompilerParams(has_side_effects=True),
    )(gin, gw, gs)
    return gin, gw.transpose(0, 2, 1, 3), gs


def solution(mesh):
    return jax.shard_map(
        local,
        mesh=mesh,
        in_specs=(P(None, "dp", "seq", None), P("dp", "seq", None), P(), P()),
        out_specs=(P("dp", "seq", None), P(None, "seq", None, "dp"), P()),
        check_vma=False,
    )
```

```python
import functools
import math

import jax
import jax.numpy as jnp
from jax import lax
from jax.experimental import pallas as pl
from jax.experimental.pallas import tpu as pltpu
from jax.sharding import PartitionSpec as P

EPS = 1e-06
F32 = jnp.float32
BF16 = jnp.bfloat16
MESH = pl.DeviceIdType.MESH

C = 768
W = 8
B = 128
DIL = (16, 32)
NX, NY, NZ = 4, 4, 8
UNITS = 9
ROWS = 96
TAPS = (1, 0, 2)
K0 = math.sqrt(2.0 / math.pi)
K1 = 0.044715
SCALE = 1.0 / math.sqrt(64 * 4096)


def body(
    saved, cot, gain, weight, gin, gw, gs,
    xv, wv, c0, c1, at0, at1, gp, rstd, run, gbuf,
    csend, crecv, keep, rsend, rrecv, tbuf, ysend, yrecv, yown, zb, zs, zf, zr, zown,
    sacc, sa0, sa1, sa2,
    x1_sem, loc_sem, halo_s, halo_r, c_s, c_r, r_s, r_r, y_s, y_r, z_s, z_r, st_s, st_r,
):
    seq = lax.axis_index("seq")
    z = lax.axis_index("dp")
    c = lax.rem(seq, 2)
    x = lax.rem(lax.div(seq, 2), NX)
    y = lax.div(seq, 2 * NX)
    cots = (c0, c1)
    ats = (at0, at1)

    def sid(yy, xx, cc):
        return (yy * NX + xx) * 2 + cc

    def rdma(src, dst, ssem, rsem, to_seq=None, to_z=None):
        where = {"seq": seq if to_seq is None else to_seq, "dp": z if to_z is None else to_z}
        return pltpu.make_async_remote_copy(
            src_ref=src, dst_ref=dst, send_sem=ssem, recv_sem=rsem, device_id=where, device_id_type=MESH
        )

    right = lax.rem(seq + 1, 32)
    left = lax.rem(seq + 31, 32)

    ld_x1 = [pltpu.make_async_copy(saved.at[1, w], xv.at[1, w], x1_sem.at[w]) for w in range(W)]
    ld_x0 = pltpu.make_async_copy(saved.at[0], xv.at[0], loc_sem.at[0])
    ld_c = pltpu.make_async_copy(cot, c1.at[:, pl.ds(DIL[1], B), :], loc_sem.at[2])
    ld_w = [pltpu.make_async_copy(weight.at[l], wv.at[l], loc_sem.at[3 + l]) for l in range(2)]
    for ld in ld_x1:
        ld.start()
    ld_c.start()

    def plane(o):
        return sid(lax.rem(y + o // NX, NY), lax.rem(x + o % NX, NX), c)

    bar = pltpu.get_barrier_semaphore()
    peers = [(sid(y, x, 1 - c), z), (lax.rem(seq + 2 * c + 31, 32), z)]
    peers += [(plane(o), z) for o in range(1, NX * NY)]
    peers += [(seq, lax.rem(z + o, NZ)) for o in range(1, NZ)]
    for s, zz in peers:
        pl.semaphore_signal(bar, inc=1, device_id={"seq": s, "dp": zz}, device_id_type=MESH)
    pl.semaphore_wait(bar, len(peers))

    def halo1():
        d = DIL[1]
        return (
            rdma(cot.at[:, pl.ds(0, d), :], c1.at[:, pl.ds(B + d, d), :], halo_s.at[0], halo_r.at[0], to_seq=left),
            rdma(cot.at[:, pl.ds(B - d, d), :], c1.at[:, pl.ds(0, d), :], halo_s.at[1], halo_r.at[1], to_seq=right),
        )

    def halo0(m):
        d = DIL[0]
        ws = pl.ds(2 * m, 2)
        return (
            rdma(c0.at[ws, pl.ds(d, d), :], c0.at[ws, pl.ds(B + d, d), :], halo_s.at[2 + 2 * m], halo_r.at[2 + 2 * m], to_seq=left),
            rdma(c0.at[ws, pl.ds(B, d), :], c0.at[ws, pl.ds(0, d), :], halo_s.at[3 + 2 * m], halo_r.at[3 + 2 * m], to_seq=right),
        )

    def clear_ends(l):
        d = DIL[l]
        zero = jnp.zeros((W, d, C), BF16)

        @pl.when(seq == 0)
        def _():
            cots[l][:, pl.ds(0, d), :] = zero

        @pl.when(seq == 31)
        def _():
            cots[l][:, pl.ds(B + d, d), :] = zero

    for h in halo1():
        h.start()

    def forward(l, w):
        xt = xv[l, w].astype(F32)
        g = gain[pl.ds(l, 1), :]
        inv = lax.rsqrt(jnp.mean(xt * xt, axis=-1, keepdims=True) + EPS)
        rstd[l, w] = jnp.broadcast_to(inv, (B, 128))
        u = xt * inv * g
        u2 = u * u
        t = jnp.tanh(u * (K0 + (K0 * K1) * u2))
        h = 0.5 + 0.5 * t
        act = u * h
        gp[l, w] = h + act * (1.0 - h) * (2.0 * K0 + (6.0 * K0 * K1) * u2)
        a = act.T
        cols = pl.ds(pl.multiple_of(w * B, B), B)
        for cc in range(2):
            for t_ in range(2):
                parts = []
                for dest in range(4):
                    for other in range(4):
                        yy, xx = (other, dest) if t_ == 0 else (dest, other)
                        r0 = sid(yy, xx, cc) * 24
                        parts.append(a[r0 : r0 + 24])
                ats[l][t_, cc, :, cols] = jnp.concatenate(parts, axis=0).astype(BF16)

    def kind(l, u):
        return lax.rem(u + (1 - l), 2)

    along_x = [seq] + [sid(y, lax.rem(x + o, NX), c) for o in range(1, NX)]
    along_y = [seq] + [sid(lax.rem(y + o, NY), x, c) for o in range(1, NY)]
    along_z = [lax.rem(z + o, NZ) for o in range(NZ)]
    twin = seq + 1 - 2 * c

    def near(t, o):
        return jnp.where(t == 0, along_x[o], along_y[o])

    def far(t, o):
        return jnp.where(t == 0, along_y[o], along_x[o])

    def tap_of(u):
        return 2 - lax.rem(lax.div(u, 3) + 1, 3)

    def core_copy(l, u):
        return rdma(csend.at[l, u], crecv.at[l, u], c_s.at[l, u], c_r.at[l, u], to_seq=twin)

    def ring_copy(l, u, o):
        return rdma(
            rsend.at[l, u, o - 1], rrecv.at[l, u, o - 1], r_s.at[l, u, o - 1], r_r.at[l, u, o - 1], to_seq=near(kind(l, u), o)
        )

    def far_copy(l, u, o):
        return rdma(ysend.at[l, u, o - 1], yrecv.at[l, u, o - 1], y_s.at[l, u, o - 1], y_r.at[l, u, o - 1], to_seq=far(kind(l, u), o))

    def z_copy(l, g, o):
        to = along_z[o]
        return rdma(zs.at[l, g, to], zr.at[l, g, o - 1], z_s.at[l, g, o - 1], z_r.at[l, g, o - 1], to_z=to)

    def stage_a(l, u, beside=None):
        d = DIL[l]
        t = kind(l, u)
        off = pl.multiple_of(lax.rem(lax.div(u, 3) + 1, 3) * d, 16)
        n0 = pl.multiple_of(lax.rem(u, 3) * 256, 256)
        rhs = cots[l][:, pl.ds(off, B), pl.ds(n0, 256)].reshape(W * B, 256)
        csend[l, u] = jnp.dot(ats[l][t, 1 - c], rhs, preferred_element_type=F32).astype(BF16)
        keep[l, u] = jnp.dot(ats[l][t, c], rhs, preferred_element_type=F32)
        if beside is not None:
            beside()
        core_copy(l, u).start()

    def stage_b(l, u):
        t = kind(l, u)
        p = jnp.where(t == 0, x, y)
        core_copy(l, u).wait_recv()

        def rows(o):
            return pl.ds(pl.multiple_of(lax.rem(p + o, 4) * ROWS, 16), ROWS)

        def total(o):
            r = rows(o)
            return keep[l, u, r, :] + crecv[l, u, r, :].astype(F32)

        for o in (2, 1, 3):
            rsend[l, u, o - 1] = total(o).astype(BF16)
            ring_copy(l, u, o).start()
        keep[l, u, rows(0), :] = total(0)

    def stage_d(l, u):
        t = kind(l, u)
        p = jnp.where(t == 0, x, y)
        q = jnp.where(t == 0, y, x)
        for o in (1, 3, 2):
            ring_copy(l, u, o).wait_recv()
        whole = keep[l, u, pl.ds(pl.multiple_of(p * ROWS, 16), ROWS), :]
        for i in range(3):
            whole = whole + rrecv[l, u, i].astype(F32)
        tbuf[...] = whole.reshape(4, 24, 256)
        for o in (2, 1, 3):
            v = tbuf[lax.rem(q + o, 4)]
            ysend[l, u, o - 1] = jnp.concatenate([v[:, :128], v[:, 128:]], axis=0).astype(BF16)
            far_copy(l, u, o).start()
        yown[u] = tbuf[q]

    def stage_e(l, u):
        for o in (1, 3, 2):
            far_copy(l, u, o).wait_recv()
        n0 = pl.multiple_of(lax.rem(u, 3) * 256, 256)
        s = yrecv[l, u, 0].astype(F32) + yrecv[l, u, 1].astype(F32) + yrecv[l, u, 2].astype(F32)
        zb[tap_of(u), :, pl.ds(n0, 256)] = yown[u] + jnp.concatenate([s[:24], s[24:]], axis=1)

    def stage_z(l, g):
        v = zb[TAPS[g]]
        for zz in range(NZ):
            part = jnp.concatenate([v[:, zz * 96 : zz * 96 + 96], jnp.zeros((24, 32), F32)], axis=1)
            zf[zz] = part
            zs[l, g, zz] = jnp.concatenate([part, jnp.zeros((8, 128), F32)], axis=0).astype(BF16)
        for o in (4, 3, 5, 2, 6, 1, 7):
            z_copy(l, g, o).start()
        zown[l, g] = zf[z]

    def stage_last(l, g):
        for o in (1, 7, 2, 6, 3, 5, 4):
            z_copy(l, g, o).wait_recv()
        tot = zown[l, g]
        for o in range(1, NZ):
            tot = tot + zr[l, g, o - 1].astype(F32)[:24]
        gw[l, TAPS[g]] = (tot * SCALE)[:, :96]

    def matmul(l, m):
        d = DIL[l]
        for n in range(3):
            acc = None
            for k in range(3):
                lhs = cots[l][pl.ds(2 * m, 2), pl.ds((2 - k) * d, B), :].reshape(2 * B, C)
                part = lax.dot_general(
                    lhs, wv[l, k, n * 256 : n * 256 + 256, :], (((1,), (1,)), ((), ())), preferred_element_type=F32
                )
                acc = part if acc is None else acc + part
            gbuf[:, n * 256 : n * 256 + 256] = acc

    def backward(l, m):
        g = gain[pl.ds(l, 1), :]
        for half in range(2):
            w = 2 * m + half
            for q in range(2):
                r = pl.ds(q * 64, 64)
                ga = gbuf[half * 128 + q * 64 : half * 128 + q * 64 + 64, :]
                inv = rstd[l, w, r, :][:, :1]
                n = xv[l, w, r, :].astype(F32) * inv
                du = ga * gp[l, w, r, :]
                sacc[l] += (du * n).reshape(8, 8, C).sum(axis=0)
                dn = du * g
                mean = jnp.mean(dn * n, axis=-1, keepdims=True)
                dx = inv * (dn - n * mean)
                if l == 1:
                    ct = c1[w, pl.ds(DIL[1] + q * 64, 64), :].astype(F32)
                    sacc[3] += ct.reshape(8, 8, C).sum(axis=0)
                    new = ct + dx
                    run[w, r, :] = new
                    nb = new.astype(BF16)
                    c0[w, pl.ds(DIL[0] + q * 64, 64), :] = nb
                    sacc[2] += nb.astype(F32).reshape(8, 8, C).sum(axis=0)
                else:
                    gin[w, r, :] = (run[w, r, :] + dx).astype(BF16)

    bufs = (sa0, sa1, sa2)
    places = (c, y * NX + x, z)
    counts = (2, NX * NY, NZ)
    first = (0, 1, NX * NY)

    def stat_copy(e, ax, o, sending):
        lo, cnt = ((0, 1), (1, 3))[e]
        if ax == 0:
            to, back = dict(to_seq=sid(y, x, 1 - c)), 1 - c
        elif ax == 1:
            to = dict(to_seq=plane(o))
            back = lax.rem(y + NY - o // NX, NY) * NX + lax.rem(x + NX - o % NX, NX)
        else:
            to, back = dict(to_z=lax.rem(z + o, NZ)), lax.rem(z + NZ - o, NZ)
        ref = bufs[ax].at[places[ax] if sending else back, pl.ds(lo, cnt)]
        i = first[ax] + o - 1
        return rdma(ref, ref, st_s.at[e, i], st_r.at[e, i], **to)

    def stat_put(e):
        for i in ((0,), (1, 2, 3))[e]:
            v = jnp.sum(sacc[i], axis=0, keepdims=True)
            sa0[c, i] = jnp.zeros((8, 128), F32)
            for j in range(6):
                sa0[c, i, j : j + 1, :] = v[:, j * 128 : j * 128 + 128]

    def stat_send(e, ax):
        for o in range(1, counts[ax]):
            stat_copy(e, ax, o, True).start()

    def stat_recv(e, ax):
        for o in range(1, counts[ax]):
            stat_copy(e, ax, o, False).wait_recv()
        lo, cnt = ((0, 1), (1, 3))[e]
        tot = bufs[ax][0, lo : lo + cnt]
        for i in range(1, counts[ax]):
            tot = tot + bufs[ax][i, lo : lo + cnt]
        if ax < 2:
            bufs[ax + 1][places[ax + 1], lo : lo + cnt] = tot
        else:
            tot = tot * SCALE
            for i in range(cnt):
                a, b = ((0, 0), (0, 1), (1, 0), (1, 1))[lo + i]
                for j in range(6):
                    gs[a, b : b + 1, j * 128 : j * 128 + 128] = tot[i, j : j + 1, :]

    sacc[...] = jnp.zeros_like(sacc)
    ld_x0.start()

    @pl.loop(0, W)
    def _(w):
        pltpu.make_async_copy(saved.at[1, w], xv.at[1, w], x1_sem.at[w]).wait()
        forward(1, w)

    ld_w[1].start()
    ld_w[0].start()
    ld_c.wait()
    ld_x0.wait()

    @pl.loop(0, 3)
    def _(u):
        stage_a(1, u, lambda: forward(0, u))

    for h in halo1():
        h.wait_recv()
    clear_ends(1)

    @pl.loop(3, 6)
    def _(u):
        stage_a(1, u, lambda: forward(0, u))
        stage_b(1, u - 3)

    ld_w[1].wait()

    @pl.loop(0, 4)
    def _(m):
        matmul(1, m)
        backward(1, m)
        for h in halo0(m):
            h.start()

        @pl.loop(0, 3)
        def _(i):
            @pl.when(m == 0)
            def _():
                stage_b(1, 3 + i)

            @pl.when(m == 3)
            def _():
                stage_d(1, i)

    stat_put(1)
    stat_send(1, 0)

    @pl.loop(6, 8)
    def _(u):
        stage_a(1, u, lambda: forward(0, u))
        stage_d(1, u - 3)

    stage_a(1, 8)
    stage_d(1, 5)

    @pl.loop(0, 3)
    def _(u):
        stage_a(0, u)
        stage_b(1, 6 + u)

    stat_recv(1, 0)
    stat_send(1, 1)
    for m in range(4):
        for h in halo0(m):
            h.wait_recv()
    clear_ends(0)

    @pl.loop(3, UNITS)
    def _(u):
        stage_a(0, u)
        stage_b(0, u - 3)
        stage_e(1, u - 3)

    stage_z(1, 0)
    stage_z(1, 1)
    ld_w[0].wait()

    @pl.loop(0, 4)
    def _(m):
        matmul(0, m)
        backward(0, m)

        @pl.loop(0, 3)
        def _(i):
            @pl.when(m == 0)
            def _():
                stage_b(0, 6 + i)

            @pl.when(m == 1)
            def _():
                stage_d(1, 6 + i)

            @pl.when(m == 2)
            def _():
                stage_d(0, i)

            @pl.when(m == 3)
            def _():
                stage_e(1, 6 + i)

    stat_put(0)
    stat_send(0, 0)
    stat_recv(1, 1)
    stat_send(1, 2)
    stat_recv(0, 0)
    stat_send(0, 1)
    stage_z(1, 2)

    @pl.loop(3, UNITS)
    def _(u):
        stage_d(0, u)

    stat_recv(0, 1)
    stat_send(0, 2)
    for g in range(3):

        @pl.loop(3 * g, 3 * g + 3)
        def _(u):
            stage_e(0, u)

        stage_z(0, g)
        if g == 0:
            for k in range(3):
                stage_last(1, k)
            stat_recv(1, 2)

    stat_recv(0, 2)
    for g in range(3):
        stage_last(0, g)

    for h in halo1():
        h.wait_send()

    @pl.loop(0, 4)
    def _(m):
        for h in halo0(m):
            h.wait_send()

    for l in range(2):

        @pl.loop(0, UNITS)
        def _(u, l=l):
            core_copy(l, u).wait_send()
            for o in range(1, 4):
                ring_copy(l, u, o).wait_send()
            for o in range(1, 4):
                far_copy(l, u, o).wait_send()

        for g in range(3):
            for o in range(1, NZ):
                z_copy(l, g, o).wait_send()
    for e in range(2):
        for ax in range(3):
            for o in range(1, counts[ax]):
                stat_copy(e, ax, o, True).wait_send()


def local(saved, cotangent, gain, weight):
    wt = weight.transpose(0, 2, 1, 3)
    dma = pltpu.SemaphoreType.DMA

    vm = pltpu.VMEM
    scratch = dict(
        xv=vm((2, W, B, C), BF16),
        wv=vm((2, 3, C, C), BF16),
        c0=vm((W, B + 2 * DIL[0], C), BF16),
        c1=vm((W, B + 2 * DIL[1], C), BF16),
        at0=vm((2, 2, 384, W * B), BF16),
        at1=vm((2, 2, 384, W * B), BF16),
        gp=vm((2, W, B, C), F32),
        rstd=vm((2, W, B, 128), F32),
        run=vm((W, B, C), F32),
        gbuf=vm((2 * B, C), F32),
        csend=vm((2, UNITS, 384, 256), BF16),
        crecv=vm((2, UNITS, 384, 256), BF16),
        keep=vm((2, UNITS, 384, 256), F32),
        rsend=vm((2, UNITS, 3, ROWS, 256), BF16),
        rrecv=vm((2, UNITS, 3, ROWS, 256), BF16),
        tbuf=vm((4, 24, 256), F32),
        ysend=vm((2, UNITS, 3, 48, 128), BF16),
        yrecv=vm((2, UNITS, 3, 48, 128), BF16),
        yown=vm((UNITS, 24, 256), F32),
        zb=vm((3, 24, C), F32),
        zs=vm((2, 3, NZ, 32, 128), BF16),
        zf=vm((NZ, 24, 128), F32),
        zr=vm((2, 3, NZ - 1, 32, 128), BF16),
        zown=vm((2, 3, 24, 128), F32),
        sacc=vm((4, 8, C), F32),
        sa0=vm((2, 4, 8, 128), F32),
        sa1=vm((NX * NY, 4, 8, 128), F32),
        sa2=vm((NZ, 4, 8, 128), F32),
        x1_sem=dma((W,)),
        loc_sem=dma((5,)),
        halo_s=dma((10,)),
        halo_r=dma((10,)),
        c_s=dma((2, UNITS)),
        c_r=dma((2, UNITS)),
        r_s=dma((2, UNITS, 3)),
        r_r=dma((2, UNITS, 3)),
        y_s=dma((2, UNITS, 3)),
        y_r=dma((2, UNITS, 3)),
        z_s=dma((2, 3, NZ - 1)),
        z_r=dma((2, 3, NZ - 1)),
        st_s=dma((2, 23)),
        st_r=dma((2, 23)),
    )
    names = list(scratch)

    def kernel(*refs):
        named = dict(zip(names, refs[7:]))
        body(*refs[:7], **named)

    gin, gw, gs = pl.pallas_call(
        kernel,
        out_shape=(
            vm((W, B, C), BF16),
            vm((2, 3, 24, 96), F32),
            vm((2, 2, C), F32),
        ),
        in_specs=[
            pl.BlockSpec(memory_space=pl.ANY),
            pl.BlockSpec(memory_space=pl.ANY),
            pl.BlockSpec(memory_space=pltpu.VMEM),
            pl.BlockSpec(memory_space=pl.ANY),
        ],
        out_specs=(
            pl.BlockSpec(memory_space=pltpu.VMEM),
            pl.BlockSpec(memory_space=pltpu.VMEM),
            pl.BlockSpec(memory_space=pltpu.VMEM),
        ),
        scratch_shapes=list(scratch.values()),
        compiler_params=pltpu.CompilerParams(
            collective_id=0, has_side_effects=True, vmem_limit_bytes=56 * 1024 * 1024
        ),
        cost_estimate=pl.CostEstimate(flops=14_500_000_000, bytes_accessed=13_000_000, transcendentals=1_600_000),
    )(saved, cotangent, gain, wt)
    return gin, gw.transpose(0, 2, 1, 3), gs


def solution(mesh):
    return jax.shard_map(
        local,
        mesh=mesh,
        in_specs=(P(None, "dp", "seq", None), P("dp", "seq", None), P(), P()),
        out_specs=(P("dp", "seq", None), P(None, "seq", None, "dp"), P()),
        check_vma=False,
    )
```

```python
import functools
import math

import jax
import jax.numpy as jnp
from jax import lax
from jax.experimental import pallas as pl
from jax.experimental.pallas import tpu as pltpu
from jax.sharding import PartitionSpec as P

EPS = 1e-06
F32 = jnp.float32
BF16 = jnp.bfloat16
MESH = pl.DeviceIdType.MESH

C = 768
W = 8
B = 128
DIL = (16, 32)
NX, NY, NZ = 4, 4, 8
UNITS = 9
ROWS = 96
TAPS = (1, 0, 2)
K0 = math.sqrt(2.0 / math.pi)
K1 = 0.044715
SCALE = 1.0 / math.sqrt(64 * 4096)


def body(
    saved, cot, gain, weight, gin, gw, gs,
    xv, wv, c0, c1, at0, at1, gp, rstd, run, gbuf,
    csend, crecv, keep, rsend, rrecv, tbuf, ysend, yrecv, yown, zb, zs, zf, zr, zown,
    sacc, sa0, sa1,
    x1_sem, loc_sem, halo_s, halo_r, c_s, c_r, r_s, r_r, y_s, y_r, z_s, z_r, st_s, st_r,
):
    seq = lax.axis_index("seq")
    z = lax.axis_index("dp")
    c = lax.rem(seq, 2)
    x = lax.rem(lax.div(seq, 2), NX)
    y = lax.div(seq, 2 * NX)
    cots = (c0, c1)
    ats = (at0, at1)

    def sid(yy, xx, cc):
        return (yy * NX + xx) * 2 + cc

    def rdma(src, dst, ssem, rsem, to_seq=None, to_z=None):
        where = {"seq": seq if to_seq is None else to_seq, "dp": z if to_z is None else to_z}
        return pltpu.make_async_remote_copy(
            src_ref=src, dst_ref=dst, send_sem=ssem, recv_sem=rsem, device_id=where, device_id_type=MESH
        )

    right = lax.rem(seq + 1, 32)
    left = lax.rem(seq + 31, 32)

    ld_x1 = [pltpu.make_async_copy(saved.at[1, w], xv.at[1, w], x1_sem.at[w]) for w in range(W)]
    ld_x0 = pltpu.make_async_copy(saved.at[0], xv.at[0], loc_sem.at[0])
    ld_c = pltpu.make_async_copy(cot, c1.at[:, pl.ds(DIL[1], B), :], loc_sem.at[2])
    ld_w = [pltpu.make_async_copy(weight.at[l], wv.at[l], loc_sem.at[3 + l]) for l in range(2)]
    for ld in ld_x1:
        ld.start()
    ld_c.start()

    def plane(o):
        return sid(lax.rem(y + o // NX, NY), lax.rem(x + o % NX, NX), c)

    bar = pltpu.get_barrier_semaphore()
    peers = [(sid(y, x, 1 - c), z), (lax.rem(seq + 2 * c + 31, 32), z)]
    peers += [(plane(o), z) for o in range(1, NX * NY)]
    peers += [(seq, lax.rem(z + o, NZ)) for o in range(1, NZ)]
    peers += [(sid(y, x, 1 - c), lax.rem(z + o, NZ)) for o in range(1, NZ)]
    for s, zz in peers:
        pl.semaphore_signal(bar, inc=1, device_id={"seq": s, "dp": zz}, device_id_type=MESH)
    pl.semaphore_wait(bar, len(peers))

    def halo1():
        d = DIL[1]
        return (
            rdma(cot.at[:, pl.ds(0, d), :], c1.at[:, pl.ds(B + d, d), :], halo_s.at[0], halo_r.at[0], to_seq=left),
            rdma(cot.at[:, pl.ds(B - d, d), :], c1.at[:, pl.ds(0, d), :], halo_s.at[1], halo_r.at[1], to_seq=right),
        )

    def halo0(m):
        d = DIL[0]
        ws = pl.ds(2 * m, 2)
        return (
            rdma(c0.at[ws, pl.ds(d, d), :], c0.at[ws, pl.ds(B + d, d), :], halo_s.at[2 + 2 * m], halo_r.at[2 + 2 * m], to_seq=left),
            rdma(c0.at[ws, pl.ds(B, d), :], c0.at[ws, pl.ds(0, d), :], halo_s.at[3 + 2 * m], halo_r.at[3 + 2 * m], to_seq=right),
        )

    def clear_ends(l):
        d = DIL[l]
        zero = jnp.zeros((W, d, C), BF16)

        @pl.when(seq == 0)
        def _():
            cots[l][:, pl.ds(0, d), :] = zero

        @pl.when(seq == 31)
        def _():
            cots[l][:, pl.ds(B + d, d), :] = zero

    for h in halo1():
        h.start()

    def forward(l, w):
        xt = xv[l, w].astype(F32)
        g = gain[pl.ds(l, 1), :]
        inv = lax.rsqrt(jnp.mean(xt * xt, axis=-1, keepdims=True) + EPS)
        rstd[l, w] = jnp.broadcast_to(inv, (B, 128))
        u = xt * inv * g
        u2 = u * u
        t = jnp.tanh(u * (K0 + (K0 * K1) * u2))
        h = 0.5 + 0.5 * t
        act = u * h
        gp[l, w] = h + act * (1.0 - h) * (2.0 * K0 + (6.0 * K0 * K1) * u2)
        a = act.T
        cols = pl.ds(pl.multiple_of(w * B, B), B)
        for cc in range(2):
            for t_ in range(2):
                parts = []
                for dest in range(4):
                    for other in range(4):
                        yy, xx = (other, dest) if t_ == 0 else (dest, other)
                        r0 = sid(yy, xx, cc) * 24
                        parts.append(a[r0 : r0 + 24])
                ats[l][t_, cc, :, cols] = jnp.concatenate(parts, axis=0).astype(BF16)

    def kind(l, u):
        return lax.rem(u + (1 - l), 2)

    along_x = [seq] + [sid(y, lax.rem(x + o, NX), c) for o in range(1, NX)]
    along_y = [seq] + [sid(lax.rem(y + o, NY), x, c) for o in range(1, NY)]
    along_z = [lax.rem(z + o, NZ) for o in range(NZ)]
    twin = seq + 1 - 2 * c

    def near(t, o):
        return jnp.where(t == 0, along_x[o], along_y[o])

    def far(t, o):
        return jnp.where(t == 0, along_y[o], along_x[o])

    def tap_of(u):
        return 2 - lax.rem(lax.div(u, 3) + 1, 3)

    def core_copy(l, u):
        return rdma(csend.at[l, u], crecv.at[l, u], c_s.at[l, u], c_r.at[l, u], to_seq=twin)

    def ring_copy(l, u, o):
        return rdma(
            rsend.at[l, u, o - 1], rrecv.at[l, u, o - 1], r_s.at[l, u, o - 1], r_r.at[l, u, o - 1], to_seq=near(kind(l, u), o)
        )

    def far_copy(l, u, o):
        return rdma(ysend.at[l, u, o - 1], yrecv.at[l, u, o - 1], y_s.at[l, u, o - 1], y_r.at[l, u, o - 1], to_seq=far(kind(l, u), o))

    def z_copy(l, g, o):
        to = along_z[o]
        return rdma(zs.at[l, g, to], zr.at[l, g, o - 1], z_s.at[l, g, o - 1], z_r.at[l, g, o - 1], to_z=to)

    def stage_a(l, u, *beside):
        d = DIL[l]
        t = kind(l, u)
        off = pl.multiple_of(lax.rem(lax.div(u, 3) + 1, 3) * d, 16)
        n0 = pl.multiple_of(lax.rem(u, 3) * 256, 256)
        rhs = cots[l][:, pl.ds(off, B), pl.ds(n0, 256)].reshape(W * B, 256)
        csend[l, u] = jnp.dot(ats[l][t, 1 - c], rhs, preferred_element_type=F32).astype(BF16)
        keep[l, u] = jnp.dot(ats[l][t, c], rhs, preferred_element_type=F32)
        for also in beside:
            also()
        core_copy(l, u).start()

    def b_wait(l, u):
        core_copy(l, u).wait_recv()

    def b_work(l, u):
        t = kind(l, u)
        p = jnp.where(t == 0, x, y)

        def rows(o):
            return pl.ds(pl.multiple_of(lax.rem(p + o, 4) * ROWS, 16), ROWS)

        def total(o):
            r = rows(o)
            return keep[l, u, r, :] + crecv[l, u, r, :].astype(F32)

        for o in (2, 1, 3):
            rsend[l, u, o - 1] = total(o).astype(BF16)
        keep[l, u, rows(0), :] = total(0)

    def b_send(l, u):
        for o in (2, 1, 3):
            ring_copy(l, u, o).start()

    def stage_b(l, u):
        b_wait(l, u)
        b_work(l, u)
        b_send(l, u)

    def stage_d(l, u):
        t = kind(l, u)
        p = jnp.where(t == 0, x, y)
        q = jnp.where(t == 0, y, x)
        for o in (1, 3, 2):
            ring_copy(l, u, o).wait_recv()
        whole = keep[l, u, pl.ds(pl.multiple_of(p * ROWS, 16), ROWS), :]
        for i in range(3):
            whole = whole + rrecv[l, u, i].astype(F32)
        tbuf[...] = whole.reshape(4, 24, 256)
        for o in (2, 1, 3):
            v = tbuf[lax.rem(q + o, 4)]
            ysend[l, u, o - 1] = jnp.concatenate([v[:, :128], v[:, 128:]], axis=0).astype(BF16)
            far_copy(l, u, o).start()
        yown[u] = tbuf[q]

    def e_wait(l, u):
        for o in (1, 3, 2):
            far_copy(l, u, o).wait_recv()

    def e_work(l, u):
        n0 = pl.multiple_of(lax.rem(u, 3) * 256, 256)
        s = yrecv[l, u, 0].astype(F32) + yrecv[l, u, 1].astype(F32) + yrecv[l, u, 2].astype(F32)
        zb[tap_of(u), :, pl.ds(n0, 256)] = yown[u] + jnp.concatenate([s[:24], s[24:]], axis=1)

    def stage_e(l, u):
        e_wait(l, u)
        e_work(l, u)

    def stage_z(l, g):
        v = zb[TAPS[g]]
        for zz in range(NZ):
            part = jnp.concatenate([v[:, zz * 96 : zz * 96 + 96], jnp.zeros((24, 32), F32)], axis=1)
            zf[zz] = part
            zs[l, g, zz] = jnp.concatenate([part, jnp.zeros((8, 128), F32)], axis=0).astype(BF16)
        for o in (4, 3, 5, 2, 6, 1, 7):
            z_copy(l, g, o).start()
        zown[l, g] = zf[z]

    def stage_last(l, g):
        for o in (1, 7, 2, 6, 3, 5, 4):
            z_copy(l, g, o).wait_recv()
        tot = zown[l, g]
        for o in range(1, NZ):
            tot = tot + zr[l, g, o - 1].astype(F32)[:24]
        gw[l, TAPS[g]] = (tot * SCALE)[:, :96]

    def matmul(l, m):
        d = DIL[l]
        for n in range(3):
            acc = None
            for k in range(3):
                lhs = cots[l][pl.ds(2 * m, 2), pl.ds((2 - k) * d, B), :].reshape(2 * B, C)
                part = lax.dot_general(
                    lhs, wv[l, k, n * 256 : n * 256 + 256, :], (((1,), (1,)), ((), ())), preferred_element_type=F32
                )
                acc = part if acc is None else acc + part
            gbuf[:, n * 256 : n * 256 + 256] = acc

    def backward(l, m):
        g = gain[pl.ds(l, 1), :]
        for half in range(2):
            w = 2 * m + half
            for q in range(2):
                r = pl.ds(q * 64, 64)
                ga = gbuf[half * 128 + q * 64 : half * 128 + q * 64 + 64, :]
                inv = rstd[l, w, r, :][:, :1]
                n = xv[l, w, r, :].astype(F32) * inv
                du = ga * gp[l, w, r, :]
                sacc[l] += (du * n).reshape(8, 8, C).sum(axis=0)
                dn = du * g
                mean = jnp.mean(dn * n, axis=-1, keepdims=True)
                dx = inv * (dn - n * mean)
                if l == 1:
                    ct = c1[w, pl.ds(DIL[1] + q * 64, 64), :].astype(F32)
                    sacc[3] += ct.reshape(8, 8, C).sum(axis=0)
                    new = ct + dx
                    run[w, r, :] = new
                    nb = new.astype(BF16)
                    c0[w, pl.ds(DIL[0] + q * 64, 64), :] = nb
                    sacc[2] += nb.astype(F32).reshape(8, 8, C).sum(axis=0)
                else:
                    gin[w, r, :] = (run[w, r, :] + dx).astype(BF16)

    bufs = (sa0, sa1)
    places = (z * 2 + c, y * NX + x)
    counts = (2 * NZ, NX * NY)

    def stat_copy(e, ax, o, sending):
        lo, cnt = ((0, 1), (1, 3))[e]
        if ax == 0:
            flip, on = o % 2, o // 2
            to = dict(to_seq=twin if flip else seq, to_z=along_z[on])
            back = lax.rem(z + NZ - on, NZ) * 2 + (1 - c if flip else c)
        else:
            to = dict(to_seq=plane(o))
            back = lax.rem(y + NY - o // NX, NY) * NX + lax.rem(x + NX - o % NX, NX)
        ref = bufs[ax].at[places[ax] if sending else back, pl.ds(lo, cnt)]
        return rdma(ref, ref, st_s.at[e, ax, o - 1], st_r.at[e, ax, o - 1], **to)

    def stat_put(e):
        for i in ((0,), (1, 2, 3))[e]:
            v = jnp.sum(sacc[i], axis=0, keepdims=True)
            sa0[places[0], i] = jnp.zeros((8, 128), F32)
            for j in range(6):
                sa0[places[0], i, j : j + 1, :] = v[:, j * 128 : j * 128 + 128]

    def stat_send(e, ax):
        for o in range(1, counts[ax]):
            stat_copy(e, ax, o, True).start()

    def stat_recv(e, ax):
        for o in range(1, counts[ax]):
            stat_copy(e, ax, o, False).wait_recv()
        lo, cnt = ((0, 1), (1, 3))[e]
        tot = bufs[ax][0, lo : lo + cnt]
        for i in range(1, counts[ax]):
            tot = tot + bufs[ax][i, lo : lo + cnt]
        if ax < 1:
            bufs[ax + 1][places[ax + 1], lo : lo + cnt] = tot
        else:
            tot = tot * SCALE
            for i in range(cnt):
                a, b = ((0, 0), (0, 1), (1, 0), (1, 1))[lo + i]
                for j in range(6):
                    gs[a, b : b + 1, j * 128 : j * 128 + 128] = tot[i, j : j + 1, :]

    sacc[...] = jnp.zeros_like(sacc)
    ld_x0.start()

    @pl.loop(0, W)
    def _(w):
        pltpu.make_async_copy(saved.at[1, w], xv.at[1, w], x1_sem.at[w]).wait()
        forward(1, w)

    ld_w[1].start()
    ld_w[0].start()
    ld_c.wait()
    ld_x0.wait()

    @pl.loop(0, 3)
    def _(u):
        stage_a(1, u, lambda: forward(0, u))

    stage_b(1, 0)
    stage_b(1, 1)
    for h in halo1():
        h.wait_recv()
    clear_ends(1)

    @pl.loop(3, 8)
    def _(u):
        stage_a(1, u, lambda: forward(0, u))
        stage_b(1, u - 1)

    stage_a(1, 8)
    stage_b(1, 7)
    ld_w[1].wait()

    def thrice(stage, l, lo):
        @pl.loop(lo, lo + 3)
        def _(u):
            stage(l, u)

    @pl.loop(0, 4)
    def _(m):
        matmul(1, m)
        backward(1, m)
        for h in halo0(m):
            h.start()

        @pl.when(m == 0)
        def _():
            stage_b(1, 8)

        @pl.when(m == 3)
        def _():
            thrice(stage_d, 1, 0)

    stat_put(1)
    stat_send(1, 0)

    @pl.loop(0, 3)
    def _(u):
        stage_a(0, u)
        stage_d(1, 3 + u)

    stat_recv(1, 0)
    stat_send(1, 1)
    stage_b(0, 0)
    stage_b(0, 1)
    for m in range(4):
        for h in halo0(m):
            h.wait_recv()
    clear_ends(0)

    @pl.loop(3, UNITS)
    def _(u):
        e_wait(1, u - 3)
        stage_a(0, u, lambda: e_work(1, u - 3))
        stage_b(0, u - 1)

    stage_b(0, 8)
    stage_z(1, 0)
    stage_z(1, 1)
    ld_w[0].wait()

    @pl.loop(0, 4)
    def _(m):
        matmul(0, m)
        backward(0, m)

        @pl.when(m == 0)
        def _():
            thrice(stage_d, 1, 6)

        @pl.when(m == 2)
        def _():
            thrice(stage_e, 1, 6)

        @pl.when(m == 3)
        def _():
            thrice(stage_d, 0, 0)

    stage_z(1, 2)
    stat_put(0)
    stat_send(0, 0)

    @pl.loop(3, UNITS)
    def _(u):
        stage_d(0, u)

    stat_recv(0, 0)
    stat_send(0, 1)
    for g in range(3):

        @pl.loop(3 * g, 3 * g + 3)
        def _(u):
            stage_e(0, u)

        stage_z(0, g)
        if g == 0:
            for k in range(3):
                stage_last(1, k)
            stat_recv(1, 1)

    stat_recv(0, 1)
    for g in range(3):
        stage_last(0, g)

    for h in halo1():
        h.wait_send()

    @pl.loop(0, 4)
    def _(m):
        for h in halo0(m):
            h.wait_send()

    for l in range(2):

        @pl.loop(0, UNITS)
        def _(u, l=l):
            core_copy(l, u).wait_send()
            for o in range(1, 4):
                ring_copy(l, u, o).wait_send()
            for o in range(1, 4):
                far_copy(l, u, o).wait_send()

        for g in range(3):
            for o in range(1, NZ):
                z_copy(l, g, o).wait_send()
    for e in range(2):
        for ax in range(2):
            for o in range(1, counts[ax]):
                stat_copy(e, ax, o, True).wait_send()


def local(saved, cotangent, gain, weight):
    wt = weight.transpose(0, 2, 1, 3)
    dma = pltpu.SemaphoreType.DMA

    vm = pltpu.VMEM
    scratch = dict(
        xv=vm((2, W, B, C), BF16),
        wv=vm((2, 3, C, C), BF16),
        c0=vm((W, B + 2 * DIL[0], C), BF16),
        c1=vm((W, B + 2 * DIL[1], C), BF16),
        at0=vm((2, 2, 384, W * B), BF16),
        at1=vm((2, 2, 384, W * B), BF16),
        gp=vm((2, W, B, C), F32),
        rstd=vm((2, W, B, 128), F32),
        run=vm((W, B, C), F32),
        gbuf=vm((2 * B, C), F32),
        csend=vm((2, UNITS, 384, 256), BF16),
        crecv=vm((2, UNITS, 384, 256), BF16),
        keep=vm((2, UNITS, 384, 256), F32),
        rsend=vm((2, UNITS, 3, ROWS, 256), BF16),
        rrecv=vm((2, UNITS, 3, ROWS, 256), BF16),
        tbuf=vm((4, 24, 256), F32),
        ysend=vm((2, UNITS, 3, 48, 128), BF16),
        yrecv=vm((2, UNITS, 3, 48, 128), BF16),
        yown=vm((UNITS, 24, 256), F32),
        zb=vm((3, 24, C), F32),
        zs=vm((2, 3, NZ, 32, 128), BF16),
        zf=vm((NZ, 24, 128), F32),
        zr=vm((2, 3, NZ - 1, 32, 128), BF16),
        zown=vm((2, 3, 24, 128), F32),
        sacc=vm((4, 8, C), F32),
        sa0=vm((2 * NZ, 4, 8, 128), F32),
        sa1=vm((NX * NY, 4, 8, 128), F32),
        x1_sem=dma((W,)),
        loc_sem=dma((5,)),
        halo_s=dma((10,)),
        halo_r=dma((10,)),
        c_s=dma((2, UNITS)),
        c_r=dma((2, UNITS)),
        r_s=dma((2, UNITS, 3)),
        r_r=dma((2, UNITS, 3)),
        y_s=dma((2, UNITS, 3)),
        y_r=dma((2, UNITS, 3)),
        z_s=dma((2, 3, NZ - 1)),
        z_r=dma((2, 3, NZ - 1)),
        st_s=dma((2, 2, 15)),
        st_r=dma((2, 2, 15)),
    )
    names = list(scratch)

    def kernel(*refs):
        named = dict(zip(names, refs[7:]))
        body(*refs[:7], **named)

    gin, gw, gs = pl.pallas_call(
        kernel,
        out_shape=(
            vm((W, B, C), BF16),
            vm((2, 3, 24, 96), F32),
            vm((2, 2, C), F32),
        ),
        in_specs=[
            pl.BlockSpec(memory_space=pl.ANY),
            pl.BlockSpec(memory_space=pl.ANY),
            pl.BlockSpec(memory_space=pltpu.VMEM),
            pl.BlockSpec(memory_space=pl.ANY),
        ],
        out_specs=(
            pl.BlockSpec(memory_space=pltpu.VMEM),
            pl.BlockSpec(memory_space=pltpu.VMEM),
            pl.BlockSpec(memory_space=pltpu.VMEM),
        ),
        scratch_shapes=list(scratch.values()),
        compiler_params=pltpu.CompilerParams(
            collective_id=0, has_side_effects=True, vmem_limit_bytes=56 * 1024 * 1024
        ),
        cost_estimate=pl.CostEstimate(flops=14_500_000_000, bytes_accessed=13_000_000, transcendentals=1_600_000),
    )(saved, cotangent, gain, wt)
    return gin, gw.transpose(0, 2, 1, 3), gs


def solution(mesh):
    return jax.shard_map(
        local,
        mesh=mesh,
        in_specs=(P(None, "dp", "seq", None), P("dp", "seq", None), P(), P()),
        out_specs=(P("dp", "seq", None), P(None, "seq", None, "dp"), P()),
        check_vma=False,
    )
```

```python
import functools
import math

import jax
import jax.numpy as jnp
from jax import lax
from jax.experimental import pallas as pl
from jax.experimental.pallas import tpu as pltpu
from jax.sharding import PartitionSpec as P

EPS = 1e-06
F32 = jnp.float32
BF16 = jnp.bfloat16
MESH = pl.DeviceIdType.MESH

C = 768
W = 8
B = 128
DIL = (16, 32)
NX, NY, NZ = 4, 4, 8
UNITS = 9
ROWS = 96
TAPS = (1, 0, 2)
K0 = math.sqrt(2.0 / math.pi)
K1 = 0.044715
SCALE = 1.0 / math.sqrt(64 * 4096)


def body(
    saved, cot, gain, weight, gin, gw, gs,
    xv, wv, c0, c1, at0, at1, gp, rstd, run, gbuf,
    csend, crecv, keep, rsend, rrecv, tbuf, ysend, yrecv, yown, zb, zs, zf, zr, zown,
    sacc, sa0, sa1,
    x1_sem, loc_sem, halo_s, halo_r, c_s, c_r, r_s, r_r, y_s, y_r, z_s, z_r, st_s, st_r,
):
    seq = lax.axis_index("seq")
    z = lax.axis_index("dp")
    c = lax.rem(seq, 2)
    x = lax.rem(lax.div(seq, 2), NX)
    y = lax.div(seq, 2 * NX)
    cots = (c0, c1)
    ats = (at0, at1)

    def sid(yy, xx, cc):
        return (yy * NX + xx) * 2 + cc

    def rdma(src, dst, ssem, rsem, to_seq=None, to_z=None):
        where = {"seq": seq if to_seq is None else to_seq, "dp": z if to_z is None else to_z}
        return pltpu.make_async_remote_copy(
            src_ref=src, dst_ref=dst, send_sem=ssem, recv_sem=rsem, device_id=where, device_id_type=MESH
        )

    right = lax.rem(seq + 1, 32)
    left = lax.rem(seq + 31, 32)

    ld_x1 = [pltpu.make_async_copy(saved.at[1, w], xv.at[1, w], x1_sem.at[w]) for w in range(W)]
    ld_x0 = pltpu.make_async_copy(saved.at[0], xv.at[0], loc_sem.at[0])
    ld_c = pltpu.make_async_copy(cot, c1.at[:, pl.ds(DIL[1], B), :], loc_sem.at[2])
    ld_w = [pltpu.make_async_copy(weight.at[l], wv.at[l], loc_sem.at[3 + l]) for l in range(2)]
    for ld in ld_x1:
        ld.start()
    ld_c.start()

    def plane(o):
        return sid(lax.rem(y + o // NX, NY), lax.rem(x + o % NX, NX), c)

    bar = pltpu.get_barrier_semaphore()
    peers = [(sid(y, x, 1 - c), z), (lax.rem(seq + 2 * c + 31, 32), z)]
    peers += [(plane(o), z) for o in range(1, NX * NY)]
    peers += [(seq, lax.rem(z + o, NZ)) for o in range(1, NZ)]
    peers += [(sid(y, x, 1 - c), lax.rem(z + o, NZ)) for o in range(1, NZ)]
    for s, zz in peers:
        pl.semaphore_signal(bar, inc=1, device_id={"seq": s, "dp": zz}, device_id_type=MESH)
    pl.semaphore_wait(bar, len(peers))

    def halo1():
        d = DIL[1]
        return (
            rdma(cot.at[:, pl.ds(0, d), :], c1.at[:, pl.ds(B + d, d), :], halo_s.at[0], halo_r.at[0], to_seq=left),
            rdma(cot.at[:, pl.ds(B - d, d), :], c1.at[:, pl.ds(0, d), :], halo_s.at[1], halo_r.at[1], to_seq=right),
        )

    def halo0(m):
        d = DIL[0]
        ws = pl.ds(2 * m, 2)
        return (
            rdma(c0.at[ws, pl.ds(d, d), :], c0.at[ws, pl.ds(B + d, d), :], halo_s.at[2 + 2 * m], halo_r.at[2 + 2 * m], to_seq=left),
            rdma(c0.at[ws, pl.ds(B, d), :], c0.at[ws, pl.ds(0, d), :], halo_s.at[3 + 2 * m], halo_r.at[3 + 2 * m], to_seq=right),
        )

    def clear_ends(l):
        d = DIL[l]
        zero = jnp.zeros((W, d, C), BF16)

        @pl.when(seq == 0)
        def _():
            cots[l][:, pl.ds(0, d), :] = zero

        @pl.when(seq == 31)
        def _():
            cots[l][:, pl.ds(B + d, d), :] = zero

    for h in halo1():
        h.start()

    def forward(l, w):
        xt = xv[l, w].astype(F32)
        g = gain[pl.ds(l, 1), :]
        inv = lax.rsqrt(jnp.mean(xt * xt, axis=-1, keepdims=True) + EPS)
        rstd[l, w] = jnp.broadcast_to(inv, (B, 128))
        u = xt * inv * g
        u2 = u * u
        t = jnp.tanh(u * (K0 + (K0 * K1) * u2))
        h = 0.5 + 0.5 * t
        act = u * h
        gp[l, w] = h + act * (1.0 - h) * (2.0 * K0 + (6.0 * K0 * K1) * u2)
        a = act.T
        cols = pl.ds(pl.multiple_of(w * B, B), B)
        for cc in range(2):
            for t_ in range(2):
                parts = []
                for dest in range(4):
                    for other in range(4):
                        yy, xx = (other, dest) if t_ == 0 else (dest, other)
                        r0 = sid(yy, xx, cc) * 24
                        parts.append(a[r0 : r0 + 24])
                ats[l][t_, cc, :, cols] = jnp.concatenate(parts, axis=0).astype(BF16)

    def kind(l, u):
        return lax.rem(u + (1 - l), 2)

    along_x = [seq] + [sid(y, lax.rem(x + o, NX), c) for o in range(1, NX)]
    along_y = [seq] + [sid(lax.rem(y + o, NY), x, c) for o in range(1, NY)]
    along_z = [lax.rem(z + o, NZ) for o in range(NZ)]
    twin = seq + 1 - 2 * c

    def near(t, o):
        return jnp.where(t == 0, along_x[o], along_y[o])

    def far(t, o):
        return jnp.where(t == 0, along_y[o], along_x[o])

    def tap_of(u):
        return 2 - lax.rem(lax.div(u, 3) + 1, 3)

    def core_copy(l, u):
        return rdma(csend.at[l, u], crecv.at[l, u], c_s.at[l, u], c_r.at[l, u], to_seq=twin)

    def ring_copy(l, u, o):
        return rdma(
            rsend.at[l, u, o - 1], rrecv.at[l, u, o - 1], r_s.at[l, u, o - 1], r_r.at[l, u, o - 1], to_seq=near(kind(l, u), o)
        )

    def far_copy(l, u, o):
        return rdma(ysend.at[l, u, o - 1], yrecv.at[l, u, o - 1], y_s.at[l, u, o - 1], y_r.at[l, u, o - 1], to_seq=far(kind(l, u), o))

    def z_copy(l, g, o):
        to = along_z[o]
        return rdma(zs.at[l, g, to], zr.at[l, g, o - 1], z_s.at[l, g, o - 1], z_r.at[l, g, o - 1], to_z=to)

    def stage_a(l, u, *beside):
        d = DIL[l]
        t = kind(l, u)
        off = pl.multiple_of(lax.rem(lax.div(u, 3) + 1, 3) * d, 16)
        n0 = pl.multiple_of(lax.rem(u, 3) * 256, 256)
        rhs = cots[l][:, pl.ds(off, B), pl.ds(n0, 256)].reshape(W * B, 256)
        csend[l, u] = jnp.dot(ats[l][t, 1 - c], rhs, preferred_element_type=F32).astype(BF16)
        keep[l, u] = jnp.dot(ats[l][t, c], rhs, preferred_element_type=F32)
        for also in beside:
            also()
        core_copy(l, u).start()

    def b_wait(l, u):
        core_copy(l, u).wait_recv()

    def b_work(l, u):
        t = kind(l, u)
        p = jnp.where(t == 0, x, y)

        def rows(o):
            return pl.ds(pl.multiple_of(lax.rem(p + o, 4) * ROWS, 16), ROWS)

        def total(o):
            r = rows(o)
            return keep[l, u, r, :] + crecv[l, u, r, :].astype(F32)

        for o in (2, 1, 3):
            rsend[l, u, o - 1] = total(o).astype(BF16)
        keep[l, u, rows(0), :] = total(0)

    def b_send(l, u):
        for o in (2, 1, 3):
            ring_copy(l, u, o).start()

    def stage_b(l, u):
        b_wait(l, u)
        b_work(l, u)
        b_send(l, u)

    def stage_d(l, u):
        t = kind(l, u)
        p = jnp.where(t == 0, x, y)
        q = jnp.where(t == 0, y, x)
        for o in (1, 3, 2):
            ring_copy(l, u, o).wait_recv()
        whole = keep[l, u, pl.ds(pl.multiple_of(p * ROWS, 16), ROWS), :]
        for i in range(3):
            whole = whole + rrecv[l, u, i].astype(F32)
        tbuf[...] = whole.reshape(4, 24, 256)
        for o in (2, 1, 3):
            v = tbuf[lax.rem(q + o, 4)]
            ysend[l, u, o - 1] = jnp.concatenate([v[:, :128], v[:, 128:]], axis=0).astype(BF16)
            far_copy(l, u, o).start()
        yown[u] = tbuf[q]

    def e_wait(l, u):
        for o in (1, 3, 2):
            far_copy(l, u, o).wait_recv()

    def e_work(l, u):
        n0 = pl.multiple_of(lax.rem(u, 3) * 256, 256)
        s = yrecv[l, u, 0].astype(F32) + yrecv[l, u, 1].astype(F32) + yrecv[l, u, 2].astype(F32)
        zb[tap_of(u), :, pl.ds(n0, 256)] = yown[u] + jnp.concatenate([s[:24], s[24:]], axis=1)

    def stage_e(l, u):
        e_wait(l, u)
        e_work(l, u)

    def stage_z(l, g):
        v = zb[TAPS[g]]
        for zz in range(NZ):
            part = jnp.concatenate([v[:, zz * 96 : zz * 96 + 96], jnp.zeros((24, 32), F32)], axis=1)
            zf[zz] = part
            zs[l, g, zz] = jnp.concatenate([part, jnp.zeros((8, 128), F32)], axis=0).astype(BF16)
        for o in (4, 3, 5, 2, 6, 1, 7):
            z_copy(l, g, o).start()
        zown[l, g] = zf[z]

    def stage_last(l, g):
        for o in (1, 7, 2, 6, 3, 5, 4):
            z_copy(l, g, o).wait_recv()
        tot = zown[l, g]
        for o in range(1, NZ):
            tot = tot + zr[l, g, o - 1].astype(F32)[:24]
        gw[l, TAPS[g]] = (tot * SCALE)[:, :96]

    def matmul(l, m):
        d = DIL[l]
        for n in range(3):
            acc = None
            for k in range(3):
                lhs = cots[l][pl.ds(2 * m, 2), pl.ds((2 - k) * d, B), :].reshape(2 * B, C)
                part = lax.dot_general(
                    lhs, wv[l, k, n * 256 : n * 256 + 256, :], (((1,), (1,)), ((), ())), preferred_element_type=F32
                )
                acc = part if acc is None else acc + part
            gbuf[:, n * 256 : n * 256 + 256] = acc

    def backward(l, m):
        g = gain[pl.ds(l, 1), :]
        for half in range(2):
            w = 2 * m + half
            for q in range(2):
                r = pl.ds(q * 64, 64)
                ga = gbuf[half * 128 + q * 64 : half * 128 + q * 64 + 64, :]
                inv = rstd[l, w, r, :][:, :1]
                n = xv[l, w, r, :].astype(F32) * inv
                du = ga * gp[l, w, r, :]
                sacc[l] += (du * n).reshape(8, 8, C).sum(axis=0)
                dn = du * g
                mean = jnp.mean(dn * n, axis=-1, keepdims=True)
                dx = inv * (dn - n * mean)
                if l == 1:
                    ct = c1[w, pl.ds(DIL[1] + q * 64, 64), :].astype(F32)
                    sacc[3] += ct.reshape(8, 8, C).sum(axis=0)
                    new = ct + dx
                    run[w, r, :] = new
                    nb = new.astype(BF16)
                    c0[w, pl.ds(DIL[0] + q * 64, 64), :] = nb
                    sacc[2] += nb.astype(F32).reshape(8, 8, C).sum(axis=0)
                else:
                    gin[w, r, :] = (run[w, r, :] + dx).astype(BF16)

    bufs = (sa0, sa1)
    places = (z * 2 + c, y * NX + x)
    counts = (2 * NZ, NX * NY)

    def stat_copy(e, ax, o, sending):
        lo, cnt = ((0, 1), (1, 3))[e]
        if ax == 0:
            flip, on = o % 2, o // 2
            to = dict(to_seq=twin if flip else seq, to_z=along_z[on])
            back = lax.rem(z + NZ - on, NZ) * 2 + (1 - c if flip else c)
        else:
            to = dict(to_seq=plane(o))
            back = lax.rem(y + NY - o // NX, NY) * NX + lax.rem(x + NX - o % NX, NX)
        ref = bufs[ax].at[places[ax] if sending else back, pl.ds(lo, cnt)]
        return rdma(ref, ref, st_s.at[e, ax, o - 1], st_r.at[e, ax, o - 1], **to)

    def stat_put(e):
        for i in ((0,), (1, 2, 3))[e]:
            v = jnp.sum(sacc[i], axis=0, keepdims=True)
            sa0[places[0], i] = jnp.zeros((8, 128), F32)
            for j in range(6):
                sa0[places[0], i, j : j + 1, :] = v[:, j * 128 : j * 128 + 128]

    def stat_send(e, ax):
        for o in range(1, counts[ax]):
            stat_copy(e, ax, o, True).start()

    def stat_recv(e, ax):
        for o in range(1, counts[ax]):
            stat_copy(e, ax, o, False).wait_recv()
        lo, cnt = ((0, 1), (1, 3))[e]
        tot = bufs[ax][0, lo : lo + cnt]
        for i in range(1, counts[ax]):
            tot = tot + bufs[ax][i, lo : lo + cnt]
        if ax < 1:
            bufs[ax + 1][places[ax + 1], lo : lo + cnt] = tot
        else:
            tot = tot * SCALE
            for i in range(cnt):
                a, b = ((0, 0), (0, 1), (1, 0), (1, 1))[lo + i]
                for j in range(6):
                    gs[a, b : b + 1, j * 128 : j * 128 + 128] = tot[i, j : j + 1, :]

    sacc[...] = jnp.zeros_like(sacc)
    ld_x0.start()

    @pl.loop(0, W)
    def _(w):
        pltpu.make_async_copy(saved.at[1, w], xv.at[1, w], x1_sem.at[w]).wait()
        forward(1, w)

    ld_w[1].start()
    ld_w[0].start()
    ld_c.wait()
    ld_x0.wait()

    @pl.loop(0, 3)
    def _(u):
        stage_a(1, u, lambda: forward(0, u))

    for h in halo1():
        h.wait_recv()
    clear_ends(1)

    @pl.loop(3, 6)
    def _(u):
        b_wait(1, u - 3)
        stage_a(1, u, lambda: forward(0, u), lambda: b_work(1, u - 3))
        b_send(1, u - 3)

    ld_w[1].wait()

    def thrice(stage, l, lo):
        @pl.loop(lo, lo + 3)
        def _(u):
            stage(l, u)

    @pl.loop(0, 4)
    def _(m):
        matmul(1, m)
        backward(1, m)
        for h in halo0(m):
            h.start()

        @pl.when(m == 0)
        def _():
            thrice(stage_b, 1, 3)

        @pl.when(m == 3)
        def _():
            thrice(stage_d, 1, 0)

    stat_put(1)
    stat_send(1, 0)

    @pl.loop(6, 8)
    def _(u):
        stage_a(1, u, lambda: forward(0, u))
        stage_d(1, u - 3)

    stage_a(1, 8)
    stage_d(1, 5)

    @pl.loop(0, 3)
    def _(u):
        b_wait(1, 6 + u)
        stage_a(0, u, lambda: b_work(1, 6 + u))
        b_send(1, 6 + u)

    stat_recv(1, 0)
    stat_send(1, 1)
    for m in range(4):
        for h in halo0(m):
            h.wait_recv()
    clear_ends(0)

    @pl.loop(3, UNITS)
    def _(u):
        e_wait(1, u - 3)
        b_wait(0, u - 3)
        stage_a(0, u, lambda: b_work(0, u - 3), lambda: e_work(1, u - 3))
        b_send(0, u - 3)

    stage_b(0, 6)
    stage_z(1, 0)
    stage_b(0, 7)
    stage_z(1, 1)
    stage_b(0, 8)
    ld_w[0].wait()

    @pl.loop(0, 4)
    def _(m):
        matmul(0, m)
        backward(0, m)

        @pl.when(m == 1)
        def _():
            thrice(stage_d, 1, 6)

        @pl.when(m == 2)
        def _():
            thrice(stage_d, 0, 0)

        @pl.when(m == 3)
        def _():
            thrice(stage_e, 1, 6)

    stage_z(1, 2)
    stat_put(0)
    stat_send(0, 0)

    thrice(stage_d, 0, 3)
    stat_recv(0, 0)
    stat_send(0, 1)
    thrice(stage_d, 0, 6)
    for g in range(3):

        @pl.loop(3 * g, 3 * g + 3)
        def _(u):
            stage_e(0, u)

        stage_z(0, g)
        if g == 0:
            for k in range(3):
                stage_last(1, k)
            stat_recv(1, 1)

    stat_recv(0, 1)
    for g in range(3):
        stage_last(0, g)

    for h in halo1():
        h.wait_send()

    @pl.loop(0, 4)
    def _(m):
        for h in halo0(m):
            h.wait_send()

    for l in range(2):

        @pl.loop(0, UNITS)
        def _(u, l=l):
            core_copy(l, u).wait_send()
            for o in range(1, 4):
                ring_copy(l, u, o).wait_send()
            for o in range(1, 4):
                far_copy(l, u, o).wait_send()

        for g in range(3):
            for o in range(1, NZ):
                z_copy(l, g, o).wait_send()
    for e in range(2):
        for ax in range(2):
            for o in range(1, counts[ax]):
                stat_copy(e, ax, o, True).wait_send()


def local(saved, cotangent, gain, weight):
    wt = weight.transpose(0, 2, 1, 3)
    dma = pltpu.SemaphoreType.DMA

    vm = pltpu.VMEM
    scratch = dict(
        xv=vm((2, W, B, C), BF16),
        wv=vm((2, 3, C, C), BF16),
        c0=vm((W, B + 2 * DIL[0], C), BF16),
        c1=vm((W, B + 2 * DIL[1], C), BF16),
        at0=vm((2, 2, 384, W * B), BF16),
        at1=vm((2, 2, 384, W * B), BF16),
        gp=vm((2, W, B, C), F32),
        rstd=vm((2, W, B, 128), F32),
        run=vm((W, B, C), F32),
        gbuf=vm((2 * B, C), F32),
        csend=vm((2, UNITS, 384, 256), BF16),
        crecv=vm((2, UNITS, 384, 256), BF16),
        keep=vm((2, UNITS, 384, 256), F32),
        rsend=vm((2, UNITS, 3, ROWS, 256), BF16),
        rrecv=vm((2, UNITS, 3, ROWS, 256), BF16),
        tbuf=vm((4, 24, 256), F32),
        ysend=vm((2, UNITS, 3, 48, 128), BF16),
        yrecv=vm((2, UNITS, 3, 48, 128), BF16),
        yown=vm((UNITS, 24, 256), F32),
        zb=vm((3, 24, C), F32),
        zs=vm((2, 3, NZ, 32, 128), BF16),
        zf=vm((NZ, 24, 128), F32),
        zr=vm((2, 3, NZ - 1, 32, 128), BF16),
        zown=vm((2, 3, 24, 128), F32),
        sacc=vm((4, 8, C), F32),
        sa0=vm((2 * NZ, 4, 8, 128), F32),
        sa1=vm((NX * NY, 4, 8, 128), F32),
        x1_sem=dma((W,)),
        loc_sem=dma((5,)),
        halo_s=dma((10,)),
        halo_r=dma((10,)),
        c_s=dma((2, UNITS)),
        c_r=dma((2, UNITS)),
        r_s=dma((2, UNITS, 3)),
        r_r=dma((2, UNITS, 3)),
        y_s=dma((2, UNITS, 3)),
        y_r=dma((2, UNITS, 3)),
        z_s=dma((2, 3, NZ - 1)),
        z_r=dma((2, 3, NZ - 1)),
        st_s=dma((2, 2, 15)),
        st_r=dma((2, 2, 15)),
    )
    names = list(scratch)

    def kernel(*refs):
        named = dict(zip(names, refs[7:]))
        body(*refs[:7], **named)

    gin, gw, gs = pl.pallas_call(
        kernel,
        out_shape=(
            vm((W, B, C), BF16),
            vm((2, 3, 24, 96), F32),
            vm((2, 2, C), F32),
        ),
        in_specs=[
            pl.BlockSpec(memory_space=pl.ANY),
            pl.BlockSpec(memory_space=pl.ANY),
            pl.BlockSpec(memory_space=pltpu.VMEM),
            pl.BlockSpec(memory_space=pl.ANY),
        ],
        out_specs=(
            pl.BlockSpec(memory_space=pltpu.VMEM),
            pl.BlockSpec(memory_space=pltpu.VMEM),
            pl.BlockSpec(memory_space=pltpu.VMEM),
        ),
        scratch_shapes=list(scratch.values()),
        compiler_params=pltpu.CompilerParams(
            collective_id=0, has_side_effects=True, vmem_limit_bytes=56 * 1024 * 1024
        ),
        cost_estimate=pl.CostEstimate(flops=14_500_000_000, bytes_accessed=13_000_000, transcendentals=1_600_000),
    )(saved, cotangent, gain, wt)
    return gin, gw.transpose(0, 2, 1, 3), gs


def solution(mesh):
    return jax.shard_map(
        local,
        mesh=mesh,
        in_specs=(P(None, "dp", "seq", None), P("dp", "seq", None), P(), P()),
        out_specs=(P("dp", "seq", None), P(None, "seq", None, "dp"), P()),
        check_vma=False,
    )
```

```python
import functools
import math

import jax
import jax.numpy as jnp
from jax import lax
from jax.experimental import pallas as pl
from jax.experimental.pallas import tpu as pltpu
from jax.sharding import PartitionSpec as P

EPS = 1e-06
F32 = jnp.float32
BF16 = jnp.bfloat16
MESH = pl.DeviceIdType.MESH

C = 768
W = 8
B = 128
DIL = (16, 32)
NX, NY, NZ = 4, 4, 8
UNITS = 9
ROWS = 96
TAPS = (1, 0, 2)
K0 = math.sqrt(2.0 / math.pi)
K1 = 0.044715
SCALE = 1.0 / math.sqrt(64 * 4096)


def body(
    saved, cot, gain, weight, gin, gw, gs,
    xv, wv, c0, c1, at0, at1, gp, rstd, run, gbuf,
    csend, crecv, keep, rsend, rrecv, tbuf, ysend, yrecv, yown, zb, zs, zf, zr, zown,
    sacc, sa0, sa1, sa2,
    x1_sem, loc_sem, halo_s, halo_r, c_s, c_r, r_s, r_r, y_s, y_r, z_s, z_r, st_s, st_r,
):
    seq = lax.axis_index("seq")
    z = lax.axis_index("dp")
    c = lax.rem(seq, 2)
    x = lax.rem(lax.div(seq, 2), NX)
    y = lax.div(seq, 2 * NX)
    cots = (c0, c1)
    ats = (at0, at1)

    def sid(yy, xx, cc):
        return (yy * NX + xx) * 2 + cc

    def rdma(src, dst, ssem, rsem, to_seq=None, to_z=None):
        where = {"seq": seq if to_seq is None else to_seq, "dp": z if to_z is None else to_z}
        return pltpu.make_async_remote_copy(
            src_ref=src, dst_ref=dst, send_sem=ssem, recv_sem=rsem, device_id=where, device_id_type=MESH
        )

    right = lax.rem(seq + 1, 32)
    left = lax.rem(seq + 31, 32)

    ld_x1 = [pltpu.make_async_copy(saved.at[1, w], xv.at[1, w], x1_sem.at[w]) for w in range(W)]
    ld_x0 = pltpu.make_async_copy(saved.at[0], xv.at[0], loc_sem.at[0])
    ld_c = pltpu.make_async_copy(cot, c1.at[:, pl.ds(DIL[1], B), :], loc_sem.at[2])
    ld_w = [pltpu.make_async_copy(weight.at[l], wv.at[l], loc_sem.at[3 + l]) for l in range(2)]
    for ld in ld_x1:
        ld.start()
    ld_c.start()

    def plane(o):
        return sid(lax.rem(y + o // NX, NY), lax.rem(x + o % NX, NX), c)

    bar = pltpu.get_barrier_semaphore()
    peers = [(sid(y, x, 1 - c), z), (lax.rem(seq + 2 * c + 31, 32), z)]
    peers += [(plane(o), z) for o in range(1, NX * NY)]
    peers += [(seq, lax.rem(z + o, NZ)) for o in range(1, NZ)]
    for s, zz in peers:
        pl.semaphore_signal(bar, inc=1, device_id={"seq": s, "dp": zz}, device_id_type=MESH)
    pl.semaphore_wait(bar, len(peers))

    def halo1():
        d = DIL[1]
        return (
            rdma(cot.at[:, pl.ds(0, d), :], c1.at[:, pl.ds(B + d, d), :], halo_s.at[0], halo_r.at[0], to_seq=left),
            rdma(cot.at[:, pl.ds(B - d, d), :], c1.at[:, pl.ds(0, d), :], halo_s.at[1], halo_r.at[1], to_seq=right),
        )

    def halo0(m):
        d = DIL[0]
        ws = pl.ds(2 * m, 2)
        return (
            rdma(c0.at[ws, pl.ds(d, d), :], c0.at[ws, pl.ds(B + d, d), :], halo_s.at[2 + 2 * m], halo_r.at[2 + 2 * m], to_seq=left),
            rdma(c0.at[ws, pl.ds(B, d), :], c0.at[ws, pl.ds(0, d), :], halo_s.at[3 + 2 * m], halo_r.at[3 + 2 * m], to_seq=right),
        )

    def clear_ends(l):
        d = DIL[l]
        zero = jnp.zeros((W, d, C), BF16)

        @pl.when(seq == 0)
        def _():
            cots[l][:, pl.ds(0, d), :] = zero

        @pl.when(seq == 31)
        def _():
            cots[l][:, pl.ds(B + d, d), :] = zero

    for h in halo1():
        h.start()

    def forward(l, w):
        xt = xv[l, w].astype(F32)
        g = gain[pl.ds(l, 1), :]
        inv = lax.rsqrt(jnp.mean(xt * xt, axis=-1, keepdims=True) + EPS)
        rstd[l, w] = jnp.broadcast_to(inv, (B, 128))
        u = xt * inv * g
        u2 = u * u
        t = jnp.tanh(u * (K0 + (K0 * K1) * u2))
        h = 0.5 + 0.5 * t
        act = u * h
        gp[l, w] = h + act * (1.0 - h) * (2.0 * K0 + (6.0 * K0 * K1) * u2)
        a = act.T
        cols = pl.ds(pl.multiple_of(w * B, B), B)
        for cc in range(2):
            for t_ in range(2):
                parts = []
                for dest in range(4):
                    for other in range(4):
                        yy, xx = (other, dest) if t_ == 0 else (dest, other)
                        r0 = sid(yy, xx, cc) * 24
                        parts.append(a[r0 : r0 + 24])
                ats[l][t_, cc, :, cols] = jnp.concatenate(parts, axis=0).astype(BF16)

    def kind(l, u):
        return lax.rem(u + (1 - l), 2)

    along_x = [seq] + [sid(y, lax.rem(x + o, NX), c) for o in range(1, NX)]
    along_y = [seq] + [sid(lax.rem(y + o, NY), x, c) for o in range(1, NY)]
    along_z = [lax.rem(z + o, NZ) for o in range(NZ)]
    twin = seq + 1 - 2 * c

    def near(t, o):
        return jnp.where(t == 0, along_x[o], along_y[o])

    def far(t, o):
        return jnp.where(t == 0, along_y[o], along_x[o])

    def tap_of(u):
        return 2 - lax.rem(lax.div(u, 3) + 1, 3)

    def core_copy(l, u):
        return rdma(csend.at[l, u], crecv.at[l, u], c_s.at[l, u], c_r.at[l, u], to_seq=twin)

    def ring_copy(l, u, o):
        return rdma(
            rsend.at[l, u, o - 1], rrecv.at[l, u, o - 1], r_s.at[l, u, o - 1], r_r.at[l, u, o - 1], to_seq=near(kind(l, u), o)
        )

    def far_copy(l, u, o):
        return rdma(ysend.at[l, u, o - 1], yrecv.at[l, u, o - 1], y_s.at[l, u, o - 1], y_r.at[l, u, o - 1], to_seq=far(kind(l, u), o))

    def z_copy(l, g, o):
        to = along_z[o]
        return rdma(zs.at[l, g, to], zr.at[l, g, o - 1], z_s.at[l, g, o - 1], z_r.at[l, g, o - 1], to_z=to)

    def stage_a(l, u, beside=None):
        d = DIL[l]
        t = kind(l, u)
        off = pl.multiple_of(lax.rem(lax.div(u, 3) + 1, 3) * d, 16)
        n0 = pl.multiple_of(lax.rem(u, 3) * 256, 256)
        rhs = cots[l][:, pl.ds(off, B), pl.ds(n0, 256)].reshape(W * B, 256)
        csend[l, u] = jnp.dot(ats[l][t, 1 - c], rhs, preferred_element_type=F32).astype(BF16)
        keep[l, u] = jnp.dot(ats[l][t, c], rhs, preferred_element_type=F32)
        if beside is not None:
            beside()
        core_copy(l, u).start()

    def stage_b(l, u):
        t = kind(l, u)
        p = jnp.where(t == 0, x, y)
        core_copy(l, u).wait_recv()

        def rows(o):
            return pl.ds(pl.multiple_of(lax.rem(p + o, 4) * ROWS, 16), ROWS)

        def total(o):
            r = rows(o)
            return keep[l, u, r, :] + crecv[l, u, r, :].astype(F32)

        for o in (2, 1, 3):
            rsend[l, u, o - 1] = total(o).astype(BF16)
            ring_copy(l, u, o).start()
        keep[l, u, rows(0), :] = total(0)

    def stage_d(l, u):
        t = kind(l, u)
        p = jnp.where(t == 0, x, y)
        q = jnp.where(t == 0, y, x)
        for o in (1, 3, 2):
            ring_copy(l, u, o).wait_recv()
        whole = keep[l, u, pl.ds(pl.multiple_of(p * ROWS, 16), ROWS), :]
        for i in range(3):
            whole = whole + rrecv[l, u, i].astype(F32)
        tbuf[...] = whole.reshape(4, 24, 256)
        for o in (2, 1, 3):
            v = tbuf[lax.rem(q + o, 4)]
            ysend[l, u, o - 1] = jnp.concatenate([v[:, :128], v[:, 128:]], axis=0).astype(BF16)
            far_copy(l, u, o).start()
        yown[u] = tbuf[q]

    def stage_e(l, u):
        for o in (1, 3, 2):
            far_copy(l, u, o).wait_recv()
        n0 = pl.multiple_of(lax.rem(u, 3) * 256, 256)
        s = yrecv[l, u, 0].astype(F32) + yrecv[l, u, 1].astype(F32) + yrecv[l, u, 2].astype(F32)
        zb[tap_of(u), :, pl.ds(n0, 256)] = yown[u] + jnp.concatenate([s[:24], s[24:]], axis=1)

    def stage_z(l, g):
        v = zb[TAPS[g]]
        for zz in range(NZ):
            part = jnp.concatenate([v[:, zz * 96 : zz * 96 + 96], jnp.zeros((24, 32), F32)], axis=1)
            zf[zz] = part
            zs[l, g, zz] = jnp.concatenate([part, jnp.zeros((8, 128), F32)], axis=0).astype(BF16)
        for o in (4, 3, 5, 2, 6, 1, 7):
            z_copy(l, g, o).start()
        zown[l, g] = zf[z]

    def stage_last(l, g):
        for o in (1, 7, 2, 6, 3, 5, 4):
            z_copy(l, g, o).wait_recv()
        tot = zown[l, g]
        for o in range(1, NZ):
            tot = tot + zr[l, g, o - 1].astype(F32)[:24]
        gw[l, TAPS[g]] = (tot * SCALE)[:, :96]

    def matmul(l, m):
        d = DIL[l]
        for n in range(3):
            acc = None
            for k in range(3):
                lhs = cots[l][pl.ds(2 * m, 2), pl.ds((2 - k) * d, B), :].reshape(2 * B, C)
                part = lax.dot_general(
                    lhs, wv[l, k, n * 256 : n * 256 + 256, :], (((1,), (1,)), ((), ())), preferred_element_type=F32
                )
                acc = part if acc is None else acc + part
            gbuf[:, n * 256 : n * 256 + 256] = acc

    def backward(l, m):
        g = gain[pl.ds(l, 1), :]
        for half in range(2):
            w = 2 * m + half
            for q in range(2):
                r = pl.ds(q * 64, 64)
                ga = gbuf[half * 128 + q * 64 : half * 128 + q * 64 + 64, :]
                inv = rstd[l, w, r, :][:, :1]
                n = xv[l, w, r, :].astype(F32) * inv
                du = ga * gp[l, w, r, :]
                sacc[l] += (du * n).reshape(8, 8, C).sum(axis=0)
                dn = du * g
                mean = jnp.mean(dn * n, axis=-1, keepdims=True)
                dx = inv * (dn - n * mean)
                if l == 1:
                    ct = c1[w, pl.ds(DIL[1] + q * 64, 64), :].astype(F32)
                    sacc[3] += ct.reshape(8, 8, C).sum(axis=0)
                    new = ct + dx
                    run[w, r, :] = new
                    nb = new.astype(BF16)
                    c0[w, pl.ds(DIL[0] + q * 64, 64), :] = nb
                    sacc[2] += nb.astype(F32).reshape(8, 8, C).sum(axis=0)
                else:
                    gin[w, r, :] = (run[w, r, :] + dx).astype(BF16)

    bufs = (sa0, sa1, sa2)
    places = (c, y * NX + x, z)
    counts = (2, NX * NY, NZ)
    first = (0, 1, NX * NY)

    def stat_copy(e, ax, o, sending):
        lo, cnt = ((0, 1), (1, 3))[e]
        if ax == 0:
            to, back = dict(to_seq=sid(y, x, 1 - c)), 1 - c
        elif ax == 1:
            to = dict(to_seq=plane(o))
            back = lax.rem(y + NY - o // NX, NY) * NX + lax.rem(x + NX - o % NX, NX)
        else:
            to, back = dict(to_z=lax.rem(z + o, NZ)), lax.rem(z + NZ - o, NZ)
        ref = bufs[ax].at[places[ax] if sending else back, pl.ds(lo, cnt)]
        i = first[ax] + o - 1
        return rdma(ref, ref, st_s.at[e, i], st_r.at[e, i], **to)

    def stat_put(e):
        for i in ((0,), (1, 2, 3))[e]:
            v = jnp.sum(sacc[i], axis=0, keepdims=True)
            sa0[c, i] = jnp.zeros((8, 128), F32)
            for j in range(6):
                sa0[c, i, j : j + 1, :] = v[:, j * 128 : j * 128 + 128]

    def stat_send(e, ax):
        for o in range(1, counts[ax]):
            stat_copy(e, ax, o, True).start()

    def stat_recv(e, ax):
        for o in range(1, counts[ax]):
            stat_copy(e, ax, o, False).wait_recv()
        lo, cnt = ((0, 1), (1, 3))[e]
        tot = bufs[ax][0, lo : lo + cnt]
        for i in range(1, counts[ax]):
            tot = tot + bufs[ax][i, lo : lo + cnt]
        if ax < 2:
            bufs[ax + 1][places[ax + 1], lo : lo + cnt] = tot
        else:
            tot = tot * SCALE
            for i in range(cnt):
                a, b = ((0, 0), (0, 1), (1, 0), (1, 1))[lo + i]
                for j in range(6):
                    gs[a, b : b + 1, j * 128 : j * 128 + 128] = tot[i, j : j + 1, :]

    sacc[...] = jnp.zeros_like(sacc)
    ld_x0.start()

    @pl.loop(0, W)
    def _(w):
        pltpu.make_async_copy(saved.at[1, w], xv.at[1, w], x1_sem.at[w]).wait()
        forward(1, w)

    ld_w[1].start()
    ld_w[0].start()
    ld_c.wait()
    ld_x0.wait()

    @pl.loop(0, 3)
    def _(u):
        stage_a(1, u, lambda: forward(0, u))

    for h in halo1():
        h.wait_recv()
    clear_ends(1)

    @pl.loop(3, 6)
    def _(u):
        stage_a(1, u, lambda: forward(0, u))
        stage_b(1, u - 3)

    ld_w[1].wait()

    @pl.loop(0, 4)
    def _(m):
        matmul(1, m)
        backward(1, m)
        for h in halo0(m):
            h.start()

        @pl.loop(0, 3)
        def _(i):
            @pl.when(m == 0)
            def _():
                stage_b(1, 3 + i)

            @pl.when(m == 3)
            def _():
                stage_d(1, i)

    stat_put(1)
    stat_send(1, 0)

    @pl.loop(6, 8)
    def _(u):
        stage_a(1, u, lambda: forward(0, u))
        stage_d(1, u - 3)

    stage_a(1, 8)
    stage_d(1, 5)

    @pl.loop(0, 3)
    def _(u):
        stage_a(0, u)
        stage_b(1, 6 + u)

    stat_recv(1, 0)
    stat_send(1, 1)
    for m in range(4):
        for h in halo0(m):
            h.wait_recv()
    clear_ends(0)

    stage_a(0, 3)
    stage_e(1, 0)

    @pl.loop(4, UNITS)
    def _(u):
        stage_a(0, u)
        stage_b(0, u - 4)
        stage_e(1, u - 3)

    stage_b(0, 5)

    stage_z(1, 0)
    stage_z(1, 1)
    ld_w[0].wait()

    @pl.loop(0, 4)
    def _(m):
        matmul(0, m)
        backward(0, m)

        @pl.loop(0, 3)
        def _(i):
            @pl.when(m == 0)
            def _():
                stage_b(0, 6 + i)

            @pl.when(m == 1)
            def _():
                stage_d(1, 6 + i)

            @pl.when(m == 2)
            def _():
                stage_d(0, i)

            @pl.when(m == 3)
            def _():
                stage_e(1, 6 + i)

    stat_put(0)
    stat_send(0, 0)
    stat_recv(1, 1)
    stat_send(1, 2)
    stat_recv(0, 0)
    stat_send(0, 1)
    stage_z(1, 2)

    @pl.loop(3, UNITS)
    def _(u):
        stage_d(0, u)

    stat_recv(0, 1)
    stat_send(0, 2)
    for g in range(3):

        @pl.loop(3 * g, 3 * g + 3)
        def _(u):
            stage_e(0, u)

        stage_z(0, g)
        if g == 0:
            for k in range(3):
                stage_last(1, k)
            stat_recv(1, 2)

    stat_recv(0, 2)
    for g in range(3):
        stage_last(0, g)

    for h in halo1():
        h.wait_send()

    @pl.loop(0, 4)
    def _(m):
        for h in halo0(m):
            h.wait_send()

    for l in range(2):

        @pl.loop(0, UNITS)
        def _(u, l=l):
            core_copy(l, u).wait_send()
            for o in range(1, 4):
                ring_copy(l, u, o).wait_send()
            for o in range(1, 4):
                far_copy(l, u, o).wait_send()

        for g in range(3):
            for o in range(1, NZ):
                z_copy(l, g, o).wait_send()
    for e in range(2):
        for ax in range(3):
            for o in range(1, counts[ax]):
                stat_copy(e, ax, o, True).wait_send()


def local(saved, cotangent, gain, weight):
    wt = weight.transpose(0, 2, 1, 3)
    dma = pltpu.SemaphoreType.DMA

    vm = pltpu.VMEM
    scratch = dict(
        xv=vm((2, W, B, C), BF16),
        wv=vm((2, 3, C, C), BF16),
        c0=vm((W, B + 2 * DIL[0], C), BF16),
        c1=vm((W, B + 2 * DIL[1], C), BF16),
        at0=vm((2, 2, 384, W * B), BF16),
        at1=vm((2, 2, 384, W * B), BF16),
        gp=vm((2, W, B, C), F32),
        rstd=vm((2, W, B, 128), F32),
        run=vm((W, B, C), F32),
        gbuf=vm((2 * B, C), F32),
        csend=vm((2, UNITS, 384, 256), BF16),
        crecv=vm((2, UNITS, 384, 256), BF16),
        keep=vm((2, UNITS, 384, 256), F32),
        rsend=vm((2, UNITS, 3, ROWS, 256), BF16),
        rrecv=vm((2, UNITS, 3, ROWS, 256), BF16),
        tbuf=vm((4, 24, 256), F32),
        ysend=vm((2, UNITS, 3, 48, 128), BF16),
        yrecv=vm((2, UNITS, 3, 48, 128), BF16),
        yown=vm((UNITS, 24, 256), F32),
        zb=vm((3, 24, C), F32),
        zs=vm((2, 3, NZ, 32, 128), BF16),
        zf=vm((NZ, 24, 128), F32),
        zr=vm((2, 3, NZ - 1, 32, 128), BF16),
        zown=vm((2, 3, 24, 128), F32),
        sacc=vm((4, 8, C), F32),
        sa0=vm((2, 4, 8, 128), F32),
        sa1=vm((NX * NY, 4, 8, 128), F32),
        sa2=vm((NZ, 4, 8, 128), F32),
        x1_sem=dma((W,)),
        loc_sem=dma((5,)),
        halo_s=dma((10,)),
        halo_r=dma((10,)),
        c_s=dma((2, UNITS)),
        c_r=dma((2, UNITS)),
        r_s=dma((2, UNITS, 3)),
        r_r=dma((2, UNITS, 3)),
        y_s=dma((2, UNITS, 3)),
        y_r=dma((2, UNITS, 3)),
        z_s=dma((2, 3, NZ - 1)),
        z_r=dma((2, 3, NZ - 1)),
        st_s=dma((2, 23)),
        st_r=dma((2, 23)),
    )
    names = list(scratch)

    def kernel(*refs):
        named = dict(zip(names, refs[7:]))
        body(*refs[:7], **named)

    gin, gw, gs = pl.pallas_call(
        kernel,
        out_shape=(
            vm((W, B, C), BF16),
            vm((2, 3, 24, 96), F32),
            vm((2, 2, C), F32),
        ),
        in_specs=[
            pl.BlockSpec(memory_space=pl.ANY),
            pl.BlockSpec(memory_space=pl.ANY),
            pl.BlockSpec(memory_space=pltpu.VMEM),
            pl.BlockSpec(memory_space=pl.ANY),
        ],
        out_specs=(
            pl.BlockSpec(memory_space=pltpu.VMEM),
            pl.BlockSpec(memory_space=pltpu.VMEM),
            pl.BlockSpec(memory_space=pltpu.VMEM),
        ),
        scratch_shapes=list(scratch.values()),
        compiler_params=pltpu.CompilerParams(
            collective_id=0, has_side_effects=True, vmem_limit_bytes=56 * 1024 * 1024
        ),
        cost_estimate=pl.CostEstimate(flops=14_500_000_000, bytes_accessed=13_000_000, transcendentals=1_600_000),
    )(saved, cotangent, gain, wt)
    return gin, gw.transpose(0, 2, 1, 3), gs


def solution(mesh):
    return jax.shard_map(
        local,
        mesh=mesh,
        in_specs=(P(None, "dp", "seq", None), P("dp", "seq", None), P(), P()),
        out_specs=(P("dp", "seq", None), P(None, "seq", None, "dp"), P()),
        check_vma=False,
    )
```
